32 devices in a mesh: dp: 16 (over z, y, core), seq: 2 (over x).
Axes of the slice: x: 2, y: 2, z: 4, core: 2. Of those that a mesh axis runs over, the one named last changes fastest.
Arguments:
- latent: bfloat16 [16384, 1408], P(('dp', 'seq')), may hold values from -6 to 6
- skip_input: bfloat16 [16384, 1408], P(('dp', 'seq')), may hold values from -6 to 6
- clip_text: bfloat16 [64, 77, 1024], P('dp', None, 'seq'), may hold values from -6 to 6
- t5_text: bfloat16 [64, 256, 2048], P('dp', None, 'seq'), may hold values from -6 to 6
- bucket: int32 [16], P('dp'), may hold values from 0 to 1
- counts: int32 [64, 2], P('dp'), may hold values from 1 to 256, as said below
- language: int32 [64], P('dp'), may hold values 0 or 1
- timesteps: int32 [64], P('dp'), may hold values from 0 to 999
- cotangent: bfloat16 [16384, 1408], P(('dp', 'seq')), may hold values from -6 to 6
- skip_weight: bfloat16 [2816, 1408], P('seq'), may hold values from -0.109375 to 0.109375
- skip_gain: float32 [1408], replicated, may hold values from 0.1 to 1.9
- time_weight: bfloat16 [256, 1408], replicated, may hold values from -0.375 to 0.375
- shift_weight: bfloat16 [1408, 1408], P(None, 'seq'), may hold values from -0.15625 to 0.15625
- norm1_gain: float32 [1408], replicated, may hold values from 0.1 to 1.9
- qkv_weight: bfloat16 [1408, 3, 1408], P(None, None, 'seq'), may hold values from -0.15625 to 0.15625
- q_gain: float32 [88], replicated, may hold values from 0.1 to 1.9
- k_gain: float32 [88], replicated, may hold values from 0.1 to 1.9
- out_weight: bfloat16 [1408, 1408], P('seq'), may hold values from -2.5 to 2.5
- norm3_gain: float32 [1408], replicated, may hold values from 0.1 to 1.9
- cross_query: bfloat16 [1408, 1408], P(None, 'seq'), may hold values from -0.15625 to 0.15625
- cq_gain: float32 [88], replicated, may hold values from 0.1 to 1.9
- t5_weight: bfloat16 [2048, 1024], P('seq'), may hold values from -0.125 to 0.125
- lang_embed: bfloat16 [2, 1024], replicated, may hold values from -6 to 6
- cross_kv: bfloat16 [1024, 2, 1408], P(None, None, 'seq'), may hold values from -0.1875 to 0.1875
- ck_gain: float32 [88], replicated, may hold values from 0.1 to 1.9
- cross_out: bfloat16 [1408, 1408], P('seq'), may hold values from -1.25 to 1.25
- norm2_gain: float32 [1408], replicated, may hold values from 0.1 to 1.9
- fc1_weight: bfloat16 [1408, 6144], P(None, 'seq'), may hold values from -0.15625 to 0.15625
- fc2_weight: bfloat16 [6144, 1408], P('seq'), may hold values from -0.078125 to 0.078125
Outputs:
- block_output: bfloat16 [16384, 1408], P(('dp', 'seq'))
- grad_latent: float32 [16384, 1408], P(('dp', 'seq'))
- grad_skip_input: float32 [16384, 1408], P(('dp', 'seq'))
- grad_clip_text: float32 [64, 77, 1024], P('dp', None, 'seq')
- grad_t5_text: float32 [64, 256, 2048], P('dp', None, 'seq')
- grad_skip_weight: float32 [2816, 1408], P('seq', 'dp')
- grad_skip_gain: float32 [1408], replicated
- grad_time_weight: float32 [256, 1408], replicated
- grad_shift_weight: float32 [1408, 1408], P('dp', 'seq')
- grad_norm1_gain: float32 [1408], replicated
- grad_qkv_weight: float32 [1408, 3, 1408], P('dp', None, 'seq')
- grad_q_gain: float32 [88], replicated
- grad_k_gain: float32 [88], replicated
- grad_out_weight: float32 [1408, 1408], P('seq', 'dp')
- grad_norm3_gain: float32 [1408], replicated
- grad_cross_query: float32 [1408, 1408], P('dp', 'seq')
- grad_cq_gain: float32 [88], replicated
- grad_t5_weight: float32 [2048, 1024], P('seq', 'dp')
- grad_lang_embed: float32 [2, 1024], replicated
- grad_cross_kv: float32 [1024, 2, 1408], P('dp', None, 'seq')
- grad_ck_gain: float32 [88], replicated
- grad_cross_out: float32 [1408, 1408], P('seq', 'dp')
- grad_norm2_gain: float32 [1408], replicated
- grad_fc1_weight: float32 [1408, 6144], P('dp', 'seq')
- grad_fc2_weight: float32 [6144, 1408], P('seq', 'dp')
The draws below stay inside these ranges and needn't reach their ends.
Inputs may be any that keep to these rules, and one draw needn't show every extreme that they name: counts[i, 0] valid leading CLIP tokens of slot i (1 to 77), counts[i, 1] valid leading mT5 tokens (1 to 256); some slot has 77 CLIP tokens, some slot one, some slot 256 mT5 tokens. `bucket`: 0: the group is one image of 32 x 32 patches; 1: 4 images of half that side. `language`: 0 for English, 1 for Chinese captions. `timesteps`: diffusion timestep of a slot.
All inputs are finite; a program needn't handle non-finite values. No bound on the sum of `language` on one device may be relied on, other than what follows from the above.
Results may differ from the reference program's by a relative error of at most 0.029.
Values may be sent and summed in bfloat16 or wider, within the bound.
No kernel may reach another device: no remote copies, remote signals or barrier semaphores. Data moves between devices by JAX's collectives and lax.ppermute only.
A program may use at most 448 MiB of HBM per device.

```python
import math
import jax
import jax.numpy as jnp
from jax import lax

D = 1408
HEADS = 16
HEAD_DIM = 88
FF = 6144
CLIP_DIM = 1024
T5_DIM = 2048
CLIP_LEN = 77
T5_LEN = 256
TFREQ = 256
SIDE = 32
SMALL_PER = 4
TOKENS = 16384
SLOTS_ALL = 64
N_DP = 16


def draw_counts(key, part):
    key = jax.random.fold_in(key, 11)
    keys = jax.random.split(key, 4)
    clip_counts = jax.random.randint(keys[0], (SLOTS_ALL,), 1, CLIP_LEN + 1)
    text_counts = jax.random.randint(keys[1], (SLOTS_ALL,), 1, T5_LEN + 1)
    fullest = jax.random.randint(keys[2], (2,), 0, SLOTS_ALL)
    offset = jax.random.randint(keys[3], (), 0, SLOTS_ALL - 1)
    indices = jnp.arange(SLOTS_ALL)
    clip_counts = jnp.where(indices == fullest[0], CLIP_LEN, clip_counts)
    clip_counts = jnp.where(indices == (fullest[0] + 1 + offset) % SLOTS_ALL, 1, clip_counts)
    text_counts = jnp.where(indices == fullest[1], T5_LEN, text_counts)
    return jnp.stack([clip_counts, text_counts], 1).astype(jnp.int32)


def set_ends(drawn, rng, least, high):
    longest = drawn.shape.index(max(drawn.shape))
    spots = []
    for shift in (0, 1):
        where = [jax.random.randint(jax.random.fold_in(rng, axis), (), 0, length) for axis, length in enumerate(drawn.shape)]
        where[longest] = (where[longest] + shift) % drawn.shape[longest]
        spots.append(tuple(where))
    return drawn.at[spots[0]].set(least).at[spots[1]].set(high)


def block_scale(own_key, dims, shards, smallest, top_value):
    gain, own = 1.0, jax.random.fold_in(own_key, 6)
    for position, blocks in shards:
        draws = jnp.exp(jax.random.uniform(jax.random.fold_in(own, position), (blocks,), jnp.float32, smallest / len(shards), top_value / len(shards)))
        gain = gain * jnp.repeat(draws, dims[position] // blocks).reshape([-1 if axis == position else 1 for axis in range(len(dims))])
    return gain


def gaussian(own_key, shape, deviation, limit, cuts=(), kind=jnp.bfloat16):
    level = block_scale(own_key, shape, cuts, -0.22, 0.18) if cuts else 1.0
    drawn = jax.random.normal(own_key, shape, jnp.float32) * deviation * level
    return jnp.minimum(jnp.maximum(drawn, -limit), limit).astype(kind)


def setup_inputs(seed: int = 0) -> dict:
    key_list = jax.random.split(jax.random.key(seed), 30)
    latent = gaussian(key_list[0], (TOKENS, D), 1.0, 6.0, ((0, 32),))
    skip_input = gaussian(key_list[1], (TOKENS, D), 1.0, 6.0, ((0, 32),))
    clip_text = gaussian(key_list[2], (SLOTS_ALL, CLIP_LEN, CLIP_DIM), 1.0, 6.0, ((0, 16), (2, 2)))
    t5_text = gaussian(key_list[3], (SLOTS_ALL, T5_LEN, T5_DIM), 1.0, 6.0, ((0, 16), (2, 2)))
    bucket = set_ends(jax.random.randint(key_list[4], (N_DP,), 0, 2), jax.random.fold_in(key_list[4], 1), 0, 1).astype(jnp.int32)
    counts = draw_counts(jax.random.fold_in(key_list[29], 71), 0)
    language = set_ends((jax.random.randint(key_list[6], (SLOTS_ALL,), 0, 2) < 1).astype(jnp.int32), jax.random.fold_in(key_list[6], 1), 0, 1)
    timesteps = set_ends(jax.random.randint(key_list[7], (SLOTS_ALL,), 0, 1000), jax.random.fold_in(key_list[7], 1), 0, 999).astype(jnp.int32)
    cotangent = gaussian(key_list[8], (TOKENS, D), 1.0, 6.0, ((0, 32),))
    skip_weight = gaussian(key_list[9], (2 * D, D), (2 * D) ** -0.5, 0.109375, ((0, 2),))
    skip_gain = jnp.clip(1.0 + 0.18 * jax.random.normal(key_list[10], (D,), jnp.float32), 0.1, 1.9)
    time_weight = gaussian(key_list[11], (TFREQ, D), TFREQ ** -0.5, 0.375)
    shift_weight = gaussian(key_list[12], (D, D), D ** -0.5, 0.15625, ((1, 2),))
    norm1_gain = jnp.clip(1.0 + 0.18 * jax.random.normal(key_list[13], (D,), jnp.float32), 0.1, 1.9)
    qkv_weight = gaussian(key_list[14], (D, 3, D), D ** -0.5, 0.15625, ((2, 2),))
    q_gain = jnp.clip(1.0 + 0.18 * jax.random.normal(key_list[15], (HEAD_DIM,), jnp.float32), 0.1, 1.9)
    k_gain = jnp.clip(1.0 + 0.18 * jax.random.normal(key_list[16], (HEAD_DIM,), jnp.float32), 0.1, 1.9)
    out_weight = gaussian(key_list[17], (D, D), (max(D // 256, 1)) ** -0.5, 2.5, ((0, 2),))
    norm3_gain = jnp.clip(1.0 + 0.18 * jax.random.normal(key_list[18], (D,), jnp.float32), 0.1, 1.9)
    cross_query = gaussian(key_list[19], (D, D), D ** -0.5, 0.15625, ((1, 2),))
    cq_gain = jnp.clip(1.0 + 0.18 * jax.random.normal(key_list[20], (HEAD_DIM,), jnp.float32), 0.1, 1.9)
    t5_weight = gaussian(key_list[21], (T5_DIM, CLIP_DIM), T5_DIM ** -0.5, 0.125, ((0, 2),))
    lang_embed = gaussian(key_list[22], (2, CLIP_DIM), 1.0, 6.0)
    cross_kv = gaussian(key_list[23], (CLIP_DIM, 2, D), CLIP_DIM ** -0.5, 0.1875, ((2, 2),))
    ck_gain = jnp.clip(1.0 + 0.18 * jax.random.normal(key_list[24], (HEAD_DIM,), jnp.float32), 0.1, 1.9)
    cross_out = gaussian(key_list[25], (D, D), (max(D // 64, 1)) ** -0.5, 1.25, ((0, 2),))
    norm2_gain = jnp.clip(1.0 + 0.18 * jax.random.normal(key_list[26], (D,), jnp.float32), 0.1, 1.9)
    fc1_weight = gaussian(key_list[27], (D, FF), D ** -0.5, 0.15625, ((1, 2),))
    fc2_weight = gaussian(key_list[28], (FF, D), FF ** -0.5, 0.078125, ((0, 2),))
    return dict(latent=latent, skip_input=skip_input, clip_text=clip_text, t5_text=t5_text, bucket=bucket, counts=counts, language=language, timesteps=timesteps, cotangent=cotangent, skip_weight=skip_weight, skip_gain=skip_gain, time_weight=time_weight, shift_weight=shift_weight, norm1_gain=norm1_gain, qkv_weight=qkv_weight, q_gain=q_gain, k_gain=k_gain, out_weight=out_weight, norm3_gain=norm3_gain, cross_query=cross_query, cq_gain=cq_gain, t5_weight=t5_weight, lang_embed=lang_embed, cross_kv=cross_kv, ck_gain=ck_gain, cross_out=cross_out, norm2_gain=norm2_gain, fc1_weight=fc1_weight, fc2_weight=fc2_weight)


PRECISE = lax.Precision.HIGHEST
EPSILON = 1e-06
NEGATIVE = -1000000000.0

@jax.custom_vjp
def low(v):
    return lax.optimization_barrier(v.astype(jnp.bfloat16)).astype(jnp.float32)

@jax.custom_vjp
def low_back(v):
    return v

def low_keep(v):
    return (low(v), None)

def low_pass(kept, grad):
    return (grad,)

def back_keep(v):
    return (v, None)

def back_low(kept, grad):
    return (low(grad),)
low.defvjp(low_keep, low_pass)
low_back.defvjp(back_keep, back_low)

def layer_norm(values):
    centre = values - lax.optimization_barrier(jnp.mean(values, -1, keepdims=True))
    return centre * lax.rsqrt(lax.optimization_barrier(jnp.mean(centre * centre, -1, keepdims=True)) + EPSILON)

def gelu_tanh(values):
    return 0.5 * values * (1.0 + jnp.tanh(0.7978845608028654 * (values + 0.044715 * values * values * values)))

def timestep_features(steps, width):
    halfway = width // 2
    rates = jnp.exp(-math.log(10000.0) * jnp.arange(halfway, dtype=jnp.float32) / halfway)
    angles = steps.astype(jnp.float32)[:, None] * rates[None, :]
    return jnp.concatenate([jnp.cos(angles), jnp.sin(angles)], 1)

def token_layout(small_group, side):
    tokens_group = side * side
    indices = jnp.arange(tokens_group, dtype=jnp.int32)
    quarter = tokens_group // 4
    slot_of = jnp.where(small_group, indices // quarter, 0).astype(jnp.int32)
    within = jnp.where(small_group, indices % quarter, indices)
    across = jnp.where(small_group, side // 2, side)
    return (slot_of, within // across, within % across)

def rotary(values, rows, cols):
    quarter = values.shape[-1] // 4
    rates = jnp.exp(-math.log(10000.0) * jnp.arange(quarter, dtype=jnp.float32) / quarter)
    pieces = []
    for offset, source in ((0, rows), (2 * quarter, cols)):
        angles = source.astype(jnp.float32)[:, None] * rates[None, :]
        cosine = jnp.cos(angles)
        sine_part = jnp.sin(angles)
        leading = values[..., offset:offset + quarter]
        trailing = values[..., offset + quarter:offset + 2 * quarter]
        pieces.append(leading * cosine - trailing * sine_part)
        pieces.append(trailing * cosine + leading * sine_part)
    return jnp.concatenate(pieces, -1)

def attend(queries, key_matrix_rows, value_matrix_rows, query_segs, key_segs):
    scaling = 1.0 / math.sqrt(queries.shape[-1])
    scores = low_back(jnp.einsum('hqd,hkd->hqk', queries, key_matrix_rows, precision=PRECISE) * scaling)
    scores = jnp.where((query_segs[:, None] == key_segs[None, :])[None], scores, NEGATIVE)
    attention_probs = low(jax.nn.softmax(scores, axis=-1))
    return jnp.einsum('hqk,hkd->hqd', attention_probs, value_matrix_rows, precision=PRECISE)

def group_forward(weights, latent_rows, skip_rows, clip_rows, t5_rows, small_group, count_rows, language_rows, step_rows):
    skip_weight, skip_gain, time_weight, shift_weight, norm1_gain, qkv_weight, q_gain, k_gain, out_weight, norm3_gain, cross_query, cq_gain, t5_weight, lang_embed, cross_kv, ck_gain, cross_out, norm2_gain, fc1_weight, fc2_weight = weights
    slot_of, row_pos, col_pos = token_layout(small_group, SIDE)

    def heads_of(values):
        return values.reshape(values.shape[0], HEADS, HEAD_DIM).transpose(1, 0, 2)

    def merge_heads(values):
        return values.transpose(1, 0, 2).reshape(values.shape[1], D)
    features = low(timestep_features(step_rows, TFREQ))
    gate_in = jax.nn.silu(jnp.dot(features, time_weight, precision=PRECISE))
    shifts = low(low_back(jnp.dot(low(gate_in), shift_weight, precision=PRECISE)))
    joined = jnp.concatenate([latent_rows, skip_rows], 1)
    hidden = low_back(jnp.dot(joined, skip_weight, precision=PRECISE))
    residual_one = layer_norm(hidden) * skip_gain
    normed = low(layer_norm(residual_one) * norm1_gain + shifts[slot_of])
    qkv_rows = low_back(jnp.einsum('td,dce->tce', normed, qkv_weight, precision=PRECISE))
    queries = low(rotary(layer_norm(heads_of(qkv_rows[:, 0])) * q_gain, row_pos, col_pos))
    key_matrix_rows = low(rotary(layer_norm(heads_of(qkv_rows[:, 1])) * k_gain, row_pos, col_pos))
    value_matrix_rows = low(heads_of(qkv_rows[:, 2]))
    attended = low_back(low(attend(queries, key_matrix_rows, value_matrix_rows, slot_of, slot_of)))
    residual_two = residual_one + low_back(jnp.dot(merge_heads(attended), out_weight, precision=PRECISE))
    normed_cross = low(layer_norm(residual_two) * norm3_gain)
    cross_pre = low_back(jnp.dot(normed_cross, cross_query, precision=PRECISE))
    cross_queries = low(layer_norm(heads_of(cross_pre)) * cq_gain)
    projected = low_back(jnp.einsum('slf,fc->slc', t5_rows, t5_weight, precision=PRECISE))
    context = low(jnp.concatenate([clip_rows, projected + lang_embed[language_rows][:, None, :]], 1))
    context_kv = low_back(jnp.einsum('slc,cke->slke', context, cross_kv, precision=PRECISE))
    context_rows = SMALL_PER * (CLIP_LEN + T5_LEN)
    flat_kv = context_kv.reshape(context_rows, 2, D)
    cross_keys = low(layer_norm(heads_of(flat_kv[:, 0])) * ck_gain)
    cross_values = low(heads_of(flat_kv[:, 1]))
    positions = jnp.arange(CLIP_LEN + T5_LEN, dtype=jnp.int32)[None, :]
    visible = jnp.where(positions < CLIP_LEN, positions < count_rows[:, :1], positions - CLIP_LEN < count_rows[:, 1:])
    key_segs = jnp.where(visible, jnp.arange(SMALL_PER, dtype=jnp.int32)[:, None], -1).reshape(-1)
    crossed = low_back(low(attend(cross_queries, cross_keys, cross_values, slot_of, key_segs)))
    residual_three = residual_two + low_back(jnp.dot(merge_heads(crossed), cross_out, precision=PRECISE))
    normed_mlp = low(layer_norm(residual_three) * norm2_gain)
    expanded = low_back(jnp.dot(normed_mlp, fc1_weight, precision=PRECISE))
    activated = low(gelu_tanh(expanded))
    return residual_three + low_back(jnp.dot(activated, fc2_weight, precision=PRECISE))

def reference(latent, skip_input, clip_text, t5_text, bucket, counts, language, timesteps, cotangent, skip_weight, skip_gain, time_weight, shift_weight, norm1_gain, qkv_weight, q_gain, k_gain, out_weight, norm3_gain, cross_query, cq_gain, t5_weight, lang_embed, cross_kv, ck_gain, cross_out, norm2_gain, fc1_weight, fc2_weight):
    tokens_group = SIDE * SIDE
    floats = tuple((member.astype(jnp.float32) for member in (latent, skip_input, clip_text, t5_text, skip_weight, skip_gain, time_weight, shift_weight, norm1_gain, qkv_weight, q_gain, k_gain, out_weight, norm3_gain, cross_query, cq_gain, t5_weight, lang_embed, cross_kv, ck_gain, cross_out, norm2_gain, fc1_weight, fc2_weight)))

    def whole(*arrays):
        weights = arrays[4:]

        def one_group(group):
            latent_rows, skip_rows, clip_rows, t5_rows, bucket_one, count_rows, language_rows, step_rows = group
            return group_forward(weights, latent_rows, skip_rows, clip_rows, t5_rows, bucket_one == 1, count_rows, language_rows, step_rows)
        groups = (arrays[0].reshape(N_DP, tokens_group, D), arrays[1].reshape(N_DP, tokens_group, D), arrays[2].reshape(N_DP, SMALL_PER, CLIP_LEN, CLIP_DIM), arrays[3].reshape(N_DP, SMALL_PER, T5_LEN, T5_DIM), bucket, counts.reshape(N_DP, SMALL_PER, 2), language.reshape(N_DP, SMALL_PER), timesteps.reshape(N_DP, SMALL_PER))
        return lax.map(jax.checkpoint(one_group), groups).reshape(N_DP * tokens_group, D)
    result, pullback = jax.vjp(whole, *floats)
    grad_latent, grad_skip, grad_clip, grad_t5, grad_skip_weight, grad_skip_gain, grad_time_weight, grad_shift_weight, grad_norm1, grad_qkv, grad_q_gain, grad_k_gain, grad_out_weight, grad_norm3, grad_cross_query, grad_cq_gain, grad_t5_weight, grad_lang, grad_cross_kv, grad_ck_gain, grad_cross_out, second_norm_gradient, grad_fc1, grad_fc2 = pullback(cotangent.astype(jnp.float32))
    return (result.astype(jnp.bfloat16), grad_latent, grad_skip, grad_clip, grad_t5, grad_skip_weight, grad_skip_gain, grad_time_weight, grad_shift_weight, grad_norm1, grad_qkv, grad_q_gain, grad_k_gain, grad_out_weight, grad_norm3, grad_cross_query, grad_cq_gain, grad_t5_weight, grad_lang, grad_cross_kv, grad_ck_gain, grad_cross_out, second_norm_gradient, grad_fc1, grad_fc2)
```

```python
import functools
import math

import jax
import jax.numpy as jnp
from jax import lax
from jax.experimental import pallas as pl
from jax.experimental.pallas import tpu as pltpu
from jax.sharding import PartitionSpec as P

HEAD_DIM = 88
SIDE = 32
SMALL_PER = 4
LANES = 128
KEY_ROWS = 384

PRECISE = lax.Precision.HIGHEST
EPSILON = 1e-06
HIDE = -30000.0
SCALE = 1.0 / math.sqrt(HEAD_DIM)
QUERY_SCALE = SCALE * math.log2(math.e)
KEY_BACK = math.log(2.0)
VMEM = 56 * 1024 * 1024

ROW_TIMES_ROW = (((1,), (1,)), ((), ()))
COL_TIMES_COL = (((0,), (0,)), ((), ()))


def params(*semantics):
    return pltpu.CompilerParams(dimension_semantics=semantics, vmem_limit_bytes=VMEM)


def lanes_of(shape):
    return lax.broadcasted_iota(jnp.int32, shape, len(shape) - 1)


def widen(values):
    fill = jnp.zeros((values.shape[0], LANES - HEAD_DIM), values.dtype)
    return jnp.concatenate([values, fill], 1)


def lane_mean(values, exact):
    high = values.astype(jnp.bfloat16)
    if exact:
        low = (values - high.astype(jnp.float32)).astype(jnp.bfloat16)
        high = jnp.concatenate([high, low], 1)
    ones = jnp.full((high.shape[1], LANES), 1.0, jnp.bfloat16)
    return jnp.dot(high, ones, preferred_element_type=jnp.float32) * (1.0 / HEAD_DIM)


def head_norm(values):
    inside = lanes_of(values.shape) < HEAD_DIM
    centre = jnp.where(inside, values - lane_mean(values, True), 0.0)
    spread = lax.rsqrt(lane_mean(centre * centre, False) + EPSILON)
    return centre * spread, spread


def by_parts(ref_rows, part, body):
    def step(number, carry):
        body(pl.ds(pl.multiple_of(number * part, part), part))
        return carry

    lax.fori_loop(0, ref_rows // part, step, 0)


def turn(values, rope):
    cosine, lead, trail = rope[:, :LANES], rope[:, LANES : 2 * LANES], rope[:, 2 * LANES :]
    quarter = HEAD_DIM // 4
    ahead = pltpu.roll(values, LANES - quarter, 1)
    behind = pltpu.roll(values, quarter, 1)
    return values * cosine + ahead * lead + behind * trail


def turn_back(values, rope):
    cosine, lead, trail = rope[:, :LANES], rope[:, LANES : 2 * LANES], rope[:, 2 * LANES :]
    quarter = HEAD_DIM // 4
    ahead = pltpu.roll(values, LANES - quarter, 1)
    behind = pltpu.roll(values, quarter, 1)
    return values * cosine - ahead * lead - behind * trail


def cut_kernel(*refs, kinds, columns, roped, chained):
    pre_ref, gain_ref = refs[:2]
    place = 2
    if roped:
        rope_ref = refs[place]
        place += 1
    extras = {}
    for kind in kinds:
        if kind != "v":
            extras[kind] = refs[place]
            place += 1
    if chained:
        place += len(kinds)
    outs = refs[place:]
    part = min(64, pre_ref.shape[0])
    lane = lanes_of((part, LANES))
    ones = jnp.where((lane == HEAD_DIM) | (lane == HEAD_DIM + 1), 1.0, 0.0)

    def rows_of(span):
        rope = rope_ref[span, :] if roped else None
        for number, kind in enumerate(kinds):
            for head, offset in enumerate(columns[number]):
                values = pre_ref[span, offset : offset + HEAD_DIM].astype(jnp.float32)
                values = widen(values)
                if kind == "v":
                    outs[number][head, span, :] = (values + ones).astype(jnp.bfloat16)
                    continue
                normed, _ = head_norm(values)
                normed = normed * gain_ref[number : number + 1, :]
                if roped:
                    normed = turn(normed, rope)
                if kind == "q":
                    normed = normed * QUERY_SCALE
                outs[number][head, span, :] = (normed + extras[kind][span, :]).astype(jnp.bfloat16)

    by_parts(pre_ref.shape[0], part, rows_of)


def cut_heads(pre, gains, kinds, columns, extras, rope=None, block=0, blocks=1, earlier=None):
    rows, width = pre.shape
    tile = min(256, rows)
    tiles = rows // tile
    here = lambda i: (block * tiles + i, 0)
    operands = [pre, gains]
    in_specs = [
        pl.BlockSpec((tile, width), lambda i: (i, 0)),
        pl.BlockSpec((8, LANES), lambda i: (0, 0)),
    ]
    if rope is not None:
        operands.append(rope)
        in_specs.append(pl.BlockSpec((tile, 3 * LANES), here))
    for kind in kinds:
        if kind != "v":
            operands.append(extras[kind])
            in_specs.append(pl.BlockSpec((tile, LANES), here))
    aliases = {}
    if earlier is not None:
        for number, array in enumerate(earlier):
            aliases[len(operands)] = number
            operands.append(array)
            in_specs.append(pl.BlockSpec(memory_space=pl.ANY))
    out_shape = [
        jax.ShapeDtypeStruct((len(cols), blocks * rows, LANES), jnp.bfloat16) for cols in columns
    ]
    out_specs = [
        pl.BlockSpec((len(cols), tile, LANES), lambda i: (0, block * tiles + i, 0))
        for cols in columns
    ]
    heads = sum(len(cols) for cols in columns)
    return pl.pallas_call(
        functools.partial(
            cut_kernel,
            kinds=kinds,
            columns=columns,
            roped=rope is not None,
            chained=earlier is not None,
        ),
        grid=(tiles,),
        in_specs=in_specs,
        out_specs=out_specs,
        out_shape=out_shape,
        input_output_aliases=aliases,
        compiler_params=params("arbitrary"),
        cost_estimate=pl.CostEstimate(
            flops=heads * rows * LANES * 40,
            bytes_accessed=rows * width * 4 + heads * rows * LANES * 2,
            transcendentals=0,
        ),
        name="cut_heads",
    )(*operands)


def join_kernel(*refs, kinds, columns, roped):
    pre_ref, gain_ref = refs[:2]
    place = 2
    if roped:
        rope_ref = refs[place]
        place += 1
    grads = refs[place : place + len(kinds)]
    out_ref, sum_ref = refs[place + len(kinds) :]
    part = min(256, pre_ref.shape[0])
    inside = lanes_of((part, LANES)) < HEAD_DIM

    @pl.when(pl.program_id(0) == 0)
    def _():
        sum_ref[...] = jnp.zeros_like(sum_ref)

    def rows_of(span):
        rope = rope_ref[span, :] if roped else None
        pieces = {}
        for number, kind in enumerate(kinds):
            total = jnp.zeros((part, LANES), jnp.float32)
            for head, offset in enumerate(columns[number]):
                slope = jnp.where(inside, grads[number][head, span, :], 0.0)
                if kind != "v":
                    slope = slope * (SCALE if kind == "q" else KEY_BACK)
                    if roped:
                        slope = turn_back(slope, rope)
                    values = pre_ref[span, offset : offset + HEAD_DIM].astype(jnp.float32)
                    normed, spread = head_norm(widen(values))
                    total = total + slope * normed
                    slope = slope * gain_ref[number : number + 1, :]
                    mean = lane_mean(slope, True)
                    mixed = lane_mean(slope * normed, False)
                    slope = (slope - mean - normed * mixed) * spread
                pieces[offset] = slope[:, :HEAD_DIM]
            if kind != "v":
                sum_ref[number : number + 1, :] += jnp.sum(total, 0, keepdims=True)
        out_ref[span, :] = jnp.concatenate(
            [pieces[offset] for offset in sorted(pieces)], 1
        ).astype(jnp.bfloat16)

    by_parts(pre_ref.shape[0], part, rows_of)


def join_heads(pre, gains, kinds, columns, grads, rope=None, block=0):
    rows, width = pre.shape
    tile = min(256, rows)
    tiles = rows // tile
    operands = [pre, gains]
    in_specs = [
        pl.BlockSpec((tile, width), lambda i: (i, 0)),
        pl.BlockSpec((8, LANES), lambda i: (0, 0)),
    ]
    if rope is not None:
        operands.append(rope)
        in_specs.append(pl.BlockSpec((tile, 3 * LANES), lambda i: (block * tiles + i, 0)))
    for array in grads:
        operands.append(array)
        in_specs.append(
            pl.BlockSpec((array.shape[0], tile, LANES), lambda i: (0, block * tiles + i, 0))
        )
    heads = sum(len(cols) for cols in columns)
    return pl.pallas_call(
        functools.partial(join_kernel, kinds=kinds, columns=columns, roped=rope is not None),
        grid=(tiles,),
        in_specs=in_specs,
        out_specs=[
            pl.BlockSpec((tile, width), lambda i: (i, 0)),
            pl.BlockSpec((8, LANES), lambda i: (0, 0)),
        ],
        out_shape=[
            jax.ShapeDtypeStruct((rows, width), jnp.bfloat16),
            jax.ShapeDtypeStruct((8, LANES), jnp.float32),
        ],
        compiler_params=params("arbitrary"),
        cost_estimate=pl.CostEstimate(
            flops=heads * rows * LANES * 60,
            bytes_accessed=rows * width * 6 + heads * rows * LANES * 4,
            transcendentals=0,
        ),
        name="join_heads",
    )(*operands)


def attend_kernel(pick, q_ref, k_ref, v_ref, o_ref, qx_ref, *, steps):
    step = pl.program_id(1)
    each, rows, _ = q_ref.shape
    part = min(256, rows)
    for start in range(0, rows, part):
        span = slice(start, start + part)
        merged = []
        for head in range(each):
            queries = q_ref[head, span, :]
            scores = lax.dot_general(
                queries, k_ref[head], ROW_TIMES_ROW, preferred_element_type=jnp.float32
            )
            weights = jnp.exp2(scores).astype(jnp.bfloat16)
            outputs = jnp.dot(weights, v_ref[head], preferred_element_type=jnp.float32)
            total = outputs[:, HEAD_DIM : HEAD_DIM + 1]
            merged.append((outputs * (1.0 / total))[:, :HEAD_DIM])
            level = -jnp.log2(total)
            high = level.astype(jnp.bfloat16).astype(jnp.float32)
            lane = lanes_of(outputs.shape)
            queries = queries.astype(jnp.float32)
            queries = jnp.where(lane == HEAD_DIM + 4, high, queries)
            queries = jnp.where(lane == HEAD_DIM + 5, level - high, queries)
            qx_ref[head, span, :] = queries.astype(jnp.bfloat16)
        merged = jnp.concatenate(merged, 1).astype(jnp.bfloat16)
        width = each * HEAD_DIM
        for number in range(steps):

            @pl.when(step == number)
            def _():
                o_ref[span, number * width : (number + 1) * width] = merged


def attend(queries, keys, values, pick, tile, key_rows, block=0, blocks=1):
    heads, rows_all, _ = queries.shape
    rows = rows_all // blocks
    tiles = rows // tile
    each = 2 if heads % 2 == 0 else 1
    there = lambda i, h, pick: (h, block * tiles + i, 0)
    keyed = lambda i, h, pick: (h, pick[i], 0)
    return pl.pallas_call(
        functools.partial(attend_kernel, steps=heads // each),
        grid_spec=pltpu.PrefetchScalarGridSpec(
            num_scalar_prefetch=1,
            grid=(tiles, heads // each),
            in_specs=[
                pl.BlockSpec((each, tile, LANES), there),
                pl.BlockSpec((each, key_rows, LANES), keyed),
                pl.BlockSpec((each, key_rows, LANES), keyed),
            ],
            out_specs=[
                pl.BlockSpec((tile, heads * HEAD_DIM), lambda i, h, pick: (i, 0)),
                pl.BlockSpec((each, tile, LANES), lambda i, h, pick: (h, i, 0)),
            ],
        ),
        out_shape=[
            jax.ShapeDtypeStruct((rows, heads * HEAD_DIM), jnp.bfloat16),
            jax.ShapeDtypeStruct((heads, rows, LANES), jnp.bfloat16),
        ],
        compiler_params=params("arbitrary", "arbitrary"),
        cost_estimate=pl.CostEstimate(
            flops=4 * heads * rows * key_rows * LANES,
            bytes_accessed=heads * (3 * rows + 2 * key_rows) * LANES * 2,
            transcendentals=heads * rows * key_rows,
        ),
        name="attend",
    )(pick, queries, keys, values)


def cut_grad_kernel(*refs, heads):
    grad_ref, o_ref = refs[:2]
    out_ref = refs[-1]
    rows = grad_ref.shape[0]
    lane = lanes_of((rows, LANES))
    for head in range(heads):
        span = slice(head * HEAD_DIM, (head + 1) * HEAD_DIM)
        slope = grad_ref[:, span].astype(jnp.bfloat16).astype(jnp.float32)
        level = -jnp.sum(slope * o_ref[:, span].astype(jnp.float32), 1, keepdims=True)
        high = level.astype(jnp.bfloat16).astype(jnp.float32)
        slope = widen(slope)
        slope = jnp.where(lane == HEAD_DIM, high, slope)
        slope = jnp.where(lane == HEAD_DIM + 1, level - high, slope)
        out_ref[head] = slope.astype(jnp.bfloat16)


def cut_grad(grad, outputs, block=0, blocks=1, earlier=None):
    rows, width = grad.shape
    heads = width // HEAD_DIM
    tile = min(256, rows)
    tiles = rows // tile
    operands = [grad, outputs]
    in_specs = [pl.BlockSpec((tile, width), lambda i: (i, 0))] * 2
    aliases = {}
    if earlier is not None:
        aliases = {2: 0}
        operands.append(earlier)
        in_specs.append(pl.BlockSpec(memory_space=pl.ANY))
    return pl.pallas_call(
        functools.partial(cut_grad_kernel, heads=heads),
        grid=(tiles,),
        in_specs=in_specs,
        out_specs=pl.BlockSpec((heads, tile, LANES), lambda i: (0, block * tiles + i, 0)),
        out_shape=jax.ShapeDtypeStruct((heads, blocks * rows, LANES), jnp.bfloat16),
        input_output_aliases=aliases,
        compiler_params=params("arbitrary"),
        cost_estimate=pl.CostEstimate(
            flops=heads * rows * LANES * 10,
            bytes_accessed=rows * width * 4 + heads * rows * LANES * 2,
            transcendentals=0,
        ),
        name="cut_grad",
    )(*operands)


def attend_back_kernel(pick, q_ref, k_ref, v_ref, g_ref, dq_ref, dk_ref, dv_ref, *, key_rows):
    tile = pl.program_id(1)
    queries, keys, slopes = q_ref[0], k_ref[0], g_ref[0]
    scores = lax.dot_general(keys, queries, ROW_TIMES_ROW, preferred_element_type=jnp.float32)
    weights = jnp.exp2(scores)
    pulls = lax.dot_general(v_ref[0], slopes, ROW_TIMES_ROW, preferred_element_type=jnp.float32)
    pulls = (weights * pulls).astype(jnp.bfloat16)
    value_grad = jnp.dot(weights.astype(jnp.bfloat16), slopes, preferred_element_type=jnp.float32)
    key_grad = jnp.dot(pulls, queries, preferred_element_type=jnp.float32)
    dq_ref[0] = lax.dot_general(pulls, keys, COL_TIMES_COL, preferred_element_type=jnp.float32)

    @pl.when(tile == 0)
    def _():
        dk_ref[...] = jnp.zeros_like(dk_ref)
        dv_ref[...] = jnp.zeros_like(dv_ref)

    start = pl.multiple_of(pick[tile] * key_rows, key_rows)
    dk_ref[0, pl.ds(start, key_rows), :] += key_grad
    dv_ref[0, pl.ds(start, key_rows), :] += value_grad


def attend_back(queries, keys, values, slopes, pick, tile, key_rows):
    heads, rows, _ = queries.shape
    all_keys = keys.shape[1]
    tiles = rows // tile
    there = lambda h, i, pick: (h, i, 0)
    keyed = lambda h, i, pick: (h, pick[i], 0)
    whole = lambda h, i, pick: (h, 0, 0)
    return pl.pallas_call(
        functools.partial(attend_back_kernel, key_rows=key_rows),
        grid_spec=pltpu.PrefetchScalarGridSpec(
            num_scalar_prefetch=1,
            grid=(heads, tiles),
            in_specs=[
                pl.BlockSpec((1, tile, LANES), there),
                pl.BlockSpec((1, key_rows, LANES), keyed),
                pl.BlockSpec((1, key_rows, LANES), keyed),
                pl.BlockSpec((1, tile, LANES), there),
            ],
            out_specs=[
                pl.BlockSpec((1, tile, LANES), there),
                pl.BlockSpec((1, all_keys, LANES), whole),
                pl.BlockSpec((1, all_keys, LANES), whole),
            ],
        ),
        out_shape=[
            jax.ShapeDtypeStruct((heads, rows, LANES), jnp.float32),
            jax.ShapeDtypeStruct((heads, all_keys, LANES), jnp.float32),
            jax.ShapeDtypeStruct((heads, all_keys, LANES), jnp.float32),
        ],
        compiler_params=params("arbitrary", "arbitrary"),
        cost_estimate=pl.CostEstimate(
            flops=10 * heads * rows * key_rows * LANES,
            bytes_accessed=heads * (2 * rows + 2 * key_rows) * LANES * 2
            + heads * (rows + 2 * all_keys) * LANES * 4,
            transcendentals=heads * rows * key_rows,
        ),
        name="attend_back",
    )(pick, queries, keys, values, slopes)


def dot_rows(left, right):
    return lax.dot_general(left, right, ROW_TIMES_ROW, preferred_element_type=jnp.float32)


def dot_sum(left, right):
    return lax.dot_general(left, right, COL_TIMES_COL, preferred_element_type=jnp.float32)


def dot_plain(left, right):
    return jnp.dot(left, right, preferred_element_type=jnp.float32)


def norm_rows(values):
    centre = values - jnp.mean(values, -1, keepdims=True)
    spread = lax.rsqrt(jnp.mean(centre * centre, -1, keepdims=True) + EPSILON)
    return centre * spread, spread


def norm_back(slope, normed, spread):
    mean = jnp.mean(slope, -1, keepdims=True)
    mixed = jnp.mean(slope * normed, -1, keepdims=True)
    return (slope - mean - normed * mixed) * spread


def low(values):
    return values.astype(jnp.bfloat16)


def wide(values):
    return values.astype(jnp.float32)


def after(values, *earlier):
    return lax.optimization_barrier((values,) + earlier)[0]


def from_back(values, step):
    size = lax.axis_size("seq")
    return lax.ppermute(values, "seq", [(i, (i + step) % size) for i in range(size)])


def to_back(values, step):
    size = lax.axis_size("seq")
    return lax.ppermute(values, "seq", [(i, (i - step) % size) for i in range(size)])


def gather_blocks(values):
    return [values] + [from_back(values, step) for step in range(1, lax.axis_size("seq"))]


def sum_blocks(terms):
    total = terms[0]
    for step in range(1, len(terms)):
        total = total + wide(to_back(low(terms[step]), step))
    return total


def sum_seq(values):
    if lax.axis_size("seq") == 2:
        return values + from_back(values, 1)
    return lax.psum(values, "seq")


def gather_weight(half):
    size = lax.axis_size("seq")
    if size == 1:
        return []
    parts = lax.axis_size("dp")
    rows = half.shape[0] // parts
    piece = lax.dynamic_slice_in_dim(half, lax.axis_index("dp") * rows, rows, 0)
    return [
        lax.all_gather(from_back(piece, step), "dp", axis=0, tiled=True) for step in range(1, size)
    ]


def scatter_sum(grad):
    parts = lax.axis_size("dp")
    rows, width = grad.shape[0] // parts, grad.shape[1]
    grad = low(grad)
    top = parts.bit_length() - 2
    if parts != 2 << top or top < 1:
        return wide(lax.psum_scatter(grad, "dp", scatter_dimension=0, tiled=True))
    place = lax.axis_index("dp")
    core = place & 1
    pairs = [[i, i + 1] for i in range(0, parts, 2)]
    held = lax.psum_scatter(
        grad, "dp", scatter_dimension=0, axis_index_groups=pairs, tiled=True
    )
    held = held.reshape((2,) * (top - 1) + (2 * rows, width))
    for bit in range(1, top):
        axis = top - 1 - bit
        mine = (place >> bit) & 1
        keep = lax.dynamic_index_in_dim(held, mine, axis, False)
        send = lax.dynamic_index_in_dim(held, 1 - mine, axis, False)
        came = lax.ppermute(send, "dp", [(i, i ^ (1 << bit)) for i in range(parts)])
        held = keep + came
    senders = [i for i in range(parts) if (i >> top) != (i & 1)]
    held = held + lax.ppermute(held, "dp", [(i, i ^ (1 << top)) for i in senders])
    owners = [i for i in range(parts) if (i >> top) == (i & 1)]
    send = lax.dynamic_slice_in_dim(held, (1 - core) * rows, rows, 0)
    came = lax.ppermute(send, "dp", [(i, i ^ 1) for i in owners])
    mine = lax.dynamic_slice_in_dim(held, core * rows, rows, 0)
    return wide(jnp.where((place >> top) == core, mine, came))


def rope_table(rows, cols):
    quarter = HEAD_DIM // 4
    lane = jnp.arange(LANES, dtype=jnp.int32)
    rates = jnp.exp(
        -math.log(10000.0) * (lane % quarter).astype(jnp.float32) / quarter
    )
    angles = jnp.arange(SIDE, dtype=jnp.float32)[:, None] * rates[None, :]
    cosine, sine = jnp.cos(angles), jnp.sin(angles)
    leading = (lane // quarter) % 2 == 0
    table = jnp.concatenate(
        [cosine, jnp.where(leading, -sine, 0.0), jnp.where(leading, 0.0, sine)], 1
    )
    lane = jnp.tile(lane, 3)
    by_row = jnp.where(lane < HEAD_DIM // 2, table, 0.0)
    by_col = jnp.where((lane >= HEAD_DIM // 2) & (lane < HEAD_DIM), table, 0.0)
    spots = jnp.arange(SIDE, dtype=jnp.int32)[None, :]
    picks = jnp.concatenate([rows[:, None] == spots, cols[:, None] == spots], 1)
    return jnp.dot(
        picks.astype(jnp.float32), jnp.concatenate([by_row, by_col], 0), precision=PRECISE
    )


def extra_lanes(columns):
    lane = jnp.arange(LANES, dtype=jnp.int32)[None, :]
    table = jnp.zeros((columns[0].shape[0], LANES), jnp.float32)
    for number, column in enumerate(columns):
        table = jnp.where(lane == HEAD_DIM + number, column[:, None], table)
    return table


def gain_rows(*gains):
    stacked = jnp.stack(gains)
    return jnp.pad(stacked, ((0, 8 - len(gains)), (0, LANES - HEAD_DIM)))


def timestep_features(steps, width):
    halfway = width // 2
    rates = jnp.exp(-math.log(10000.0) * jnp.arange(halfway, dtype=jnp.float32) / halfway)
    angles = steps.astype(jnp.float32)[:, None] * rates[None, :]
    return jnp.concatenate([jnp.cos(angles), jnp.sin(angles)], 1)


def gelu_and_slope(values):
    outer = 0.7978845608028654
    inner = 0.044715
    square = values * values
    bend = jnp.tanh(outer * (values + inner * square * values))
    half = 0.5 * (1.0 + bend)
    slope = half + 0.5 * values * (1.0 - bend * bend) * outer * (1.0 + 3.0 * inner * square)
    return low(values * half), slope


def on_device(
    latent,
    skip_input,
    clip_text,
    t5_text,
    bucket,
    counts,
    language,
    timesteps,
    cotangent,
    skip_weight,
    skip_gain,
    time_weight,
    shift_weight,
    norm1_gain,
    qkv_weight,
    q_gain,
    k_gain,
    out_weight,
    norm3_gain,
    cross_query,
    cq_gain,
    t5_weight,
    lang_embed,
    cross_kv,
    ck_gain,
    cross_out,
    norm2_gain,
    fc1_weight,
    fc2_weight,
):
    size = lax.axis_size("seq")
    me = lax.axis_index("seq")
    rows, width = latent.shape
    local_width = out_weight.shape[0]
    local_heads = local_width // HEAD_DIM
    all_heads = local_heads * size
    clip_length, text_local = clip_text.shape[1:]
    text_length = t5_text.shape[1]
    text_width = lang_embed.shape[1]
    tokens = rows * size
    small = (bucket[0] == 1).astype(jnp.int32)
    quarter = tokens // SMALL_PER
    tile = min(quarter, rows)
    slots = max(1, rows // quarter)

    def owner(step):
        return (me - step) % size

    def first_slot(device):
        return small * (device * rows // quarter)

    order = jnp.concatenate(
        [owner(step) * rows + jnp.arange(rows, dtype=jnp.int32) for step in range(size)]
    )
    slot_of = jnp.where(small == 1, order // quarter, 0)
    within = jnp.where(small == 1, order % quarter, order)
    across = jnp.where(small == 1, SIDE // 2, SIDE)
    rope = rope_table(within // across, within % across)
    own_slots = slot_of[:rows]
    self_extras = dict(
        q=extra_lanes([wide(slot_of == j) for j in range(SMALL_PER)]),
        k=extra_lanes(
            [jnp.where(slot_of == j, 0.0, HIDE) for j in range(SMALL_PER)]
            + [jnp.ones((tokens,), jnp.float32)] * 2
        ),
    )

    qkv_rows = qkv_weight.transpose(1, 2, 0).reshape(3 * local_width, width)
    cq_own = cross_query.T
    kv_own = cross_kv.transpose(1, 2, 0).reshape(2 * local_width, text_width)
    skip_blocks = [skip_weight] + gather_weight(skip_weight)
    cross_blocks = [jnp.concatenate([cq_own, cross_out], 0)]
    cross_blocks += gather_weight(cross_blocks[0])
    cq_full = jnp.concatenate([block[:local_width] for block in cross_blocks], 0)
    co_full = jnp.concatenate([block[local_width:] for block in cross_blocks], 0)
    kv_full = jnp.concatenate([kv_own] + gather_weight(kv_own), 0)

    features = low(timestep_features(timesteps, time_weight.shape[0]))
    gate = low(jax.nn.silu(dot_plain(features, time_weight)))
    shift_own = low(dot_plain(gate, shift_weight))
    shift_blocks = gather_blocks(shift_own)
    if size == 2:
        shifts = jnp.where(
            me == 0,
            jnp.concatenate(shift_blocks, 1),
            jnp.concatenate(shift_blocks[::-1], 1),
        )
    else:
        shifts = lax.all_gather(shift_own, "seq", axis=1, tiled=True)
    own_pick = own_slots[:, None] == jnp.arange(SMALL_PER, dtype=jnp.int32)[None, :]
    shift_rows = dot_plain(low(own_pick), shifts)

    partial = dot_plain(t5_text.reshape(-1, t5_text.shape[2]), t5_weight)
    partial = partial.reshape(SMALL_PER, text_length, text_width)

    def slots_for(values, device):
        return lax.dynamic_slice_in_dim(values, first_slot(device), slots, 0)

    projected = sum_blocks([slots_for(partial, owner(step)) for step in range(size)])
    clip_full = jnp.zeros((slots, clip_length, text_width), jnp.bfloat16)
    for step in range(size):
        block = slots_for(clip_text, (me + step) % size if step else me)
        block = from_back(block, step) if step else block
        clip_full = lax.dynamic_update_slice_in_dim(
            clip_full, block, owner(step) * text_local, 2
        )
    my_languages = lax.dynamic_slice_in_dim(language, first_slot(me), slots, 0)
    words = wide(lang_embed)
    chosen = jnp.where((my_languages == 1)[:, None], words[1][None, :], words[0][None, :])
    spare = KEY_ROWS - text_length - clip_length
    context = jnp.concatenate(
        [
            low(projected + chosen[:, None, :]),
            clip_full,
            jnp.zeros((slots, spare, text_width), jnp.bfloat16),
        ],
        1,
    ).reshape(slots * KEY_ROWS, text_width)
    my_counts = lax.dynamic_slice_in_dim(counts, first_slot(me), slots, 0)
    key_place = jnp.arange(KEY_ROWS, dtype=jnp.int32)[None, :]
    visible = jnp.where(
        key_place < text_length,
        key_place < my_counts[:, 1:],
        (key_place - text_length < my_counts[:, :1]) & (key_place < text_length + clip_length),
    ).reshape(-1)
    cross_key_extra = jnp.where(visible, 0.0, HIDE)
    ones_keys = jnp.ones((slots * KEY_ROWS,), jnp.float32)
    zeros_keys = jnp.zeros((slots * KEY_ROWS,), jnp.float32)
    cross_extras = dict(
        q=extra_lanes([jnp.ones((rows,), jnp.float32)]),
        k=extra_lanes([cross_key_extra, zeros_keys, zeros_keys, zeros_keys, ones_keys, ones_keys]),
    )
    context_kv = dot_rows(context, kv_full)
    kv_gains = gain_rows(ck_gain, ck_gain)
    key_columns = [
        2 * local_width * group + HEAD_DIM * head
        for group in range(size)
        for head in range(local_heads)
    ]
    kv_columns = [key_columns, [column + local_width for column in key_columns]]
    cross_keys, cross_values = cut_heads(
        context_kv, kv_gains, ("k", "v"), kv_columns, cross_extras
    )

    if size == 2:
        chunk = [
            jnp.where(me == 0, latent, skip_input),
            jnp.where(me == 0, skip_input, latent),
        ]
    else:
        joined = jnp.concatenate([latent, skip_input], 1)
        part = 2 * width // size
        chunk = [
            lax.dynamic_slice_in_dim(joined, owner(step) * part, part, 1) for step in range(size)
        ]
    hidden = dot_plain(chunk[0], skip_blocks[0])
    for step in range(1, size):
        hidden = hidden + dot_plain(chunk[step], skip_blocks[step])
    skip_normed, skip_spread = norm_rows(hidden)
    residual_one = skip_normed * skip_gain
    first_normed, first_spread = norm_rows(residual_one)
    normed = low(first_normed * norm1_gain + shift_rows)
    normed_blocks = gather_blocks(normed)

    self_kinds = ("q", "k", "v")
    self_columns = [
        [local_width * which + HEAD_DIM * head for head in range(local_heads)]
        for which in range(3)
    ]
    self_gains = gain_rows(q_gain, k_gain)
    qkv_blocks, cut = [], None
    for step in range(size):
        qkv_blocks.append(dot_rows(normed_blocks[step], qkv_rows))
        cut = cut_heads(
            qkv_blocks[step],
            self_gains,
            self_kinds,
            self_columns,
            self_extras,
            rope,
            step,
            size,
            cut,
        )
    queries, keys, values = cut
    no_pick = jnp.zeros((1,), jnp.int32)
    self_outputs, self_queries = [None] * size, [None] * size
    out_terms = [None] * size
    for step in list(range(1, size)) + [0]:
        self_outputs[step], self_queries[step] = attend(
            queries, keys, values, no_pick, rows, tokens, step, size
        )
        out_terms[step] = dot_plain(self_outputs[step], out_weight)
    residual_two = residual_one + sum_blocks(out_terms)

    third_normed, third_spread = norm_rows(residual_two)
    normed_cross = low(third_normed * norm3_gain)
    cross_pre = dot_rows(normed_cross, cq_full)
    query_gains = gain_rows(cq_gain)
    query_columns = [[HEAD_DIM * head for head in range(all_heads)]]
    (cross_queries,) = cut_heads(cross_pre, query_gains, ("q",), query_columns, cross_extras)
    cross_pick = small * (jnp.arange(rows // tile, dtype=jnp.int32) * tile // quarter)
    cross_outputs, cross_queries = attend(
        cross_queries, cross_keys, cross_values, cross_pick, tile, KEY_ROWS
    )
    residual_three = residual_two + dot_plain(cross_outputs, co_full)

    second_normed, second_spread = norm_rows(residual_three)
    mlp_blocks = gather_blocks(low(second_normed * norm2_gain))
    cotangent_blocks = gather_blocks(cotangent)
    active, expanded_grads, fc_terms, mlp_terms = [], [], [], []
    for step in range(size):
        gate_out, gate_slope = gelu_and_slope(dot_plain(mlp_blocks[step], fc1_weight))
        active.append(gate_out)
        expanded_grads.append(low(dot_rows(cotangent_blocks[step], fc2_weight) * gate_slope))
        mlp_terms.append(dot_rows(expanded_grads[step], fc1_weight))
    mlp_slope = sum_blocks(mlp_terms)
    for step in range(size):
        fc_terms.append(dot_plain(active[step], fc2_weight))
    block_output = low(residual_three + sum_blocks(fc_terms))
    active_all = jnp.concatenate(active, 0)
    expanded_all = jnp.concatenate(expanded_grads, 0)
    grad_fc2 = scatter_sum(dot_sum(jnp.concatenate(cotangent_blocks, 0), active_all)).T
    grad_fc1 = scatter_sum(dot_sum(jnp.concatenate(mlp_blocks, 0), expanded_all))

    grad_norm2 = jnp.sum(mlp_slope * second_normed, 0)
    grad_three = wide(cotangent) + norm_back(
        mlp_slope * norm2_gain, second_normed, second_spread
    )

    three_low = low(grad_three)
    cross_slopes = cut_grad(low(dot_rows(three_low, co_full)), cross_outputs)
    grad_cq, grad_ck, grad_cv = attend_back(
        cross_queries, cross_keys, cross_values, cross_slopes, cross_pick, tile, KEY_ROWS
    )
    cross_pre_grad, query_sums = join_heads(
        cross_pre, query_gains, ("q",), query_columns, (grad_cq,)
    )
    cross_slope = dot_plain(cross_pre_grad, cq_full)
    grad_norm3 = jnp.sum(cross_slope * third_normed, 0)
    grad_two = grad_three + norm_back(cross_slope * norm3_gain, third_normed, third_spread)
    two_blocks = gather_blocks(low(grad_two))
    context_kv_grad, key_sums = join_heads(
        context_kv, kv_gains, ("k", "v"), kv_columns, (grad_ck, grad_cv)
    )
    context_grad = dot_plain(context_kv_grad, kv_full).reshape(slots, KEY_ROWS, text_width)

    def own_part(summed):
        blocks = [
            summed[:, step * (summed.shape[1] // size) : (step + 1) * (summed.shape[1] // size)]
            for step in range(size)
        ]
        return sum_blocks(blocks)

    grad_cross = scatter_sum(
        jnp.concatenate(
            [dot_sum(normed_cross, cross_pre_grad), dot_sum(three_low, cross_outputs)], 1
        )
    )
    grad_cross_query = own_part(grad_cross[:, : all_heads * HEAD_DIM])
    grad_cross_out = own_part(grad_cross[:, all_heads * HEAD_DIM :]).T
    grad_cross_kv = own_part(scatter_sum(dot_sum(context, context_kv_grad)))
    grad_cross_kv = grad_cross_kv.reshape(-1, 2, local_width)

    def spread_slots(blocks):
        found = []
        for slot in range(SMALL_PER):
            total = 0.0
            for step, block in enumerate(blocks):
                offset = slot - first_slot((me + step) % size)
                inside = (offset >= 0) & (offset < slots)
                part = lax.dynamic_index_in_dim(
                    block, jnp.clip(offset, 0, slots - 1), 0, False
                )
                total = total + jnp.where(inside, wide(part), 0.0)
            found.append(total)
        return jnp.stack(found)

    text_grad = context_grad[:, :text_length]
    text_low = low(text_grad)
    text_blocks = [text_low] + [to_back(text_low, step) for step in range(1, size)]
    project_all = low(spread_slots(text_blocks)).reshape(SMALL_PER * text_length, text_width)
    clip_blocks = []
    for step in range(size):
        block = lax.dynamic_slice_in_dim(
            context_grad[:, text_length : text_length + clip_length],
            owner(step) * text_local,
            text_local,
            2,
        )
        clip_blocks.append(to_back(low(block), step) if step else block)
    grad_clip = spread_slots(clip_blocks)
    grad_t5 = dot_rows(project_all, t5_weight).reshape(t5_text.shape)
    grad_t5_weight = scatter_sum(
        dot_sum(project_all, t5_text.reshape(-1, t5_text.shape[2]))
    ).T
    tongues = wide(my_languages[None, :] == jnp.arange(2, dtype=jnp.int32)[:, None])
    grad_lang = jnp.dot(tongues, jnp.sum(text_grad, 1), precision=PRECISE)

    slopes = None
    for step in range(size):
        slopes = cut_grad(
            low(dot_rows(two_blocks[step], out_weight)), self_outputs[step], step, size, slopes
        )
    self_queries = jnp.concatenate(self_queries, 1)
    back_tile = min(512, tokens)
    head_grads = attend_back(
        self_queries,
        keys,
        values,
        slopes,
        jnp.zeros((tokens // back_tile,), jnp.int32),
        back_tile,
        tokens,
    )
    qkv_grads, normed_terms = [None] * size, [None] * size
    self_sums = 0.0
    for step in list(range(1, size)) + [0]:
        qkv_grads[step], sums = join_heads(
            qkv_blocks[step], self_gains, self_kinds, self_columns, head_grads, rope, step
        )
        self_sums = self_sums + sums
        normed_terms[step] = dot_plain(qkv_grads[step], qkv_rows)
    normed_slope = sum_blocks(normed_terms)
    normed_all = jnp.concatenate(normed_blocks, 0)
    grad_qkv = scatter_sum(dot_sum(normed_all, jnp.concatenate(qkv_grads, 0)))
    grad_qkv = grad_qkv.reshape(-1, 3, local_width)
    grad_out = scatter_sum(
        dot_sum(jnp.concatenate(two_blocks, 0), jnp.concatenate(self_outputs, 0))
    ).T

    grad_norm1 = jnp.sum(normed_slope * first_normed, 0)
    residual_slope = grad_two + norm_back(normed_slope * norm1_gain, first_normed, first_spread)
    grad_skip_gain = jnp.sum(residual_slope * skip_normed, 0)
    hidden_low = low(norm_back(residual_slope * skip_gain, skip_normed, skip_spread))
    hidden_blocks = gather_blocks(hidden_low)
    joined_blocks = [chunk[0]]
    for step in range(1, size):
        if size == 2:
            block = chunk[1]
        else:
            block = lax.dynamic_slice_in_dim(joined, (me + step) % size * part, part, 1)
        joined_blocks.append(from_back(block, step))
    grad_skip_weight = scatter_sum(
        dot_sum(jnp.concatenate(hidden_blocks, 0), jnp.concatenate(joined_blocks, 0))
    ).T
    joined_grads = [dot_rows(hidden_low, block) for block in skip_blocks]
    if size == 2:
        grad_latent = jnp.where(me == 0, joined_grads[0], joined_grads[1])
        grad_skip_input = jnp.where(me == 0, joined_grads[1], joined_grads[0])
    else:
        joined_grad = jnp.zeros((rows, 2 * width), jnp.float32)
        for step in range(size):
            joined_grad = lax.dynamic_update_slice_in_dim(
                joined_grad, joined_grads[step], owner(step) * part, 1
            )
        grad_latent, grad_skip_input = joined_grad[:, :width], joined_grad[:, width:]

    shift_terms = jnp.dot(wide(own_pick).T, normed_slope, precision=PRECISE)
    shift_low = low(sum_seq(shift_terms))
    shift_all = lax.all_gather(shift_low, "dp", axis=0, tiled=True)
    steps_all = lax.all_gather(timesteps, "dp", axis=0, tiled=True)
    features_all = low(timestep_features(steps_all, time_weight.shape[0]))
    gate_all, silu_pull = jax.vjp(jax.nn.silu, dot_plain(features_all, time_weight))
    shift_mine = lax.dynamic_slice_in_dim(shift_all, me * local_width, local_width, 1)
    parts = lax.axis_size("dp")
    gate_mine = lax.dynamic_slice_in_dim(
        low(gate_all), lax.axis_index("dp") * (width // parts), width // parts, 1
    )
    grad_shift = dot_sum(gate_mine, shift_mine)
    (time_slope,) = silu_pull(sum_seq(dot_rows(shift_mine, shift_weight)))
    grad_time = jnp.dot(wide(features_all).T, time_slope, precision=PRECISE)

    gains = [
        grad_skip_gain,
        grad_norm1,
        self_sums[0, :HEAD_DIM],
        self_sums[1, :HEAD_DIM],
        grad_norm3,
        query_sums[0, :HEAD_DIM],
        key_sums[0, :HEAD_DIM],
        grad_norm2,
        grad_lang.reshape(-1),
    ]
    packed = lax.psum(jnp.concatenate(gains), ("dp", "seq"))
    totals, start = [], 0
    for gain in gains:
        totals.append(packed[start : start + gain.shape[0]])
        start += gain.shape[0]
    return (
        block_output,
        grad_latent,
        grad_skip_input,
        grad_clip,
        grad_t5,
        grad_skip_weight,
        totals[0],
        grad_time,
        grad_shift,
        totals[1],
        grad_qkv,
        totals[2],
        totals[3],
        grad_out,
        totals[4],
        grad_cross_query,
        totals[5],
        grad_t5_weight,
        totals[8].reshape(lang_embed.shape),
        grad_cross_kv,
        totals[6],
        grad_cross_out,
        totals[7],
        grad_fc1,
        grad_fc2,
    )


def solution(mesh):
    return jax.shard_map(
        on_device,
        mesh=mesh,
        in_specs=(
            P(("dp", "seq"), None),
            P(("dp", "seq"), None),
            P("dp", None, "seq"),
            P("dp", None, "seq"),
            P("dp"),
            P("dp", None),
            P("dp"),
            P("dp"),
            P(("dp", "seq"), None),
            P("seq", None),
            P(),
            P(),
            P(None, "seq"),
            P(),
            P(None, None, "seq"),
            P(),
            P(),
            P("seq", None),
            P(),
            P(None, "seq"),
            P(),
            P("seq", None),
            P(),
            P(None, None, "seq"),
            P(),
            P("seq", None),
            P(),
            P(None, "seq"),
            P("seq", None),
        ),
        out_specs=(
            P(("dp", "seq"), None),
            P(("dp", "seq"), None),
            P(("dp", "seq"), None),
            P("dp", None, "seq"),
            P("dp", None, "seq"),
            P("seq", "dp"),
            P(),
            P(),
            P("dp", "seq"),
            P(),
            P("dp", None, "seq"),
            P(),
            P(),
            P("seq", "dp"),
            P(),
            P("dp", "seq"),
            P(),
            P("seq", "dp"),
            P(),
            P("dp", None, "seq"),
            P(),
            P("seq", "dp"),
            P(),
            P("dp", "seq"),
            P("seq", "dp"),
        ),
        check_vma=False,
    )
```

```python
import functools
import math

import jax
import jax.numpy as jnp
import numpy as np
from jax import lax
from jax.experimental import pallas as pl
from jax.experimental.pallas import tpu as pltpu
from jax.sharding import PartitionSpec as P

HEAD_DIM = 88
SIDE = 32
SMALL_PER = 4
LANES = 128
KEY_ROWS = 384

PRECISE = lax.Precision.HIGHEST
EPSILON = 1e-06
HIDE = -30000.0
SCALE = 1.0 / math.sqrt(HEAD_DIM)
QUERY_SCALE = SCALE * math.log2(math.e)
KEY_BACK = math.log(2.0)
VMEM = 20 * 1024 * 1024


SCALE_FLOPS = 2e8


def effort(us):
    return pl.CostEstimate(flops=int(us * SCALE_FLOPS), bytes_accessed=1, transcendentals=0)


ROW_TIMES_ROW = (((1,), (1,)), ((), ()))
COL_TIMES_COL = (((0,), (0,)), ((), ()))


def params(*semantics):
    return pltpu.CompilerParams(dimension_semantics=semantics, vmem_limit_bytes=VMEM)


def lanes_of(shape):
    return lax.broadcasted_iota(jnp.int32, shape, len(shape) - 1)


def widen(values):
    fill = jnp.zeros((values.shape[0], LANES - HEAD_DIM), values.dtype)
    return jnp.concatenate([values, fill], 1)


def lane_mean(values, exact):
    high = values.astype(jnp.bfloat16)
    if exact:
        low = (values - high.astype(jnp.float32)).astype(jnp.bfloat16)
        high = jnp.concatenate([high, low], 1)
    ones = jnp.full((high.shape[1], LANES), 1.0, jnp.bfloat16)
    return jnp.dot(high, ones, preferred_element_type=jnp.float32) * (1.0 / HEAD_DIM)


def head_norm(values):
    inside = lanes_of(values.shape) < HEAD_DIM
    centre = jnp.where(inside, values - lane_mean(values, True), 0.0)
    spread = lax.rsqrt(lane_mean(centre * centre, False) + EPSILON)
    return centre * spread, spread


def by_parts(ref_rows, part, body):
    def step(number, carry):
        body(pl.ds(pl.multiple_of(number * part, part), part))
        return carry

    lax.fori_loop(0, ref_rows // part, step, 0)


def turn(values, rope):
    cosine, lead, trail = rope[:, :LANES], rope[:, LANES : 2 * LANES], rope[:, 2 * LANES :]
    quarter = HEAD_DIM // 4
    ahead = pltpu.roll(values, LANES - quarter, 1)
    behind = pltpu.roll(values, quarter, 1)
    return values * cosine + ahead * lead + behind * trail


def turn_back(values, rope):
    cosine, lead, trail = rope[:, :LANES], rope[:, LANES : 2 * LANES], rope[:, 2 * LANES :]
    quarter = HEAD_DIM // 4
    ahead = pltpu.roll(values, LANES - quarter, 1)
    behind = pltpu.roll(values, quarter, 1)
    return values * cosine - ahead * lead - behind * trail


def cut_kernel(*refs, kinds, columns, roped, chained):
    pre_ref, gain_ref = refs[:2]
    place = 2
    if roped:
        rope_ref = refs[place]
        place += 1
    extras = {}
    for kind in kinds:
        if kind != "v":
            extras[kind] = refs[place]
            place += 1
    if chained:
        place += len(kinds)
    outs = refs[place:]
    part = min(64, pre_ref.shape[0])
    lane = lanes_of((part, LANES))
    ones = jnp.where((lane == HEAD_DIM) | (lane == HEAD_DIM + 1), 1.0, 0.0)

    def rows_of(span):
        rope = rope_ref[span, :] if roped else None
        for number, kind in enumerate(kinds):
            for head, offset in enumerate(columns[number]):
                values = pre_ref[span, offset : offset + HEAD_DIM].astype(jnp.float32)
                values = widen(values)
                if kind == "v":
                    outs[number][head, span, :] = (values + ones).astype(jnp.bfloat16)
                    continue
                normed, _ = head_norm(values)
                normed = normed * gain_ref[number : number + 1, :]
                if roped:
                    normed = turn(normed, rope)
                if kind == "q":
                    normed = normed * QUERY_SCALE
                outs[number][head, span, :] = (normed + extras[kind][span, :]).astype(jnp.bfloat16)

    by_parts(pre_ref.shape[0], part, rows_of)


def cut_heads(pre, gains, kinds, columns, extras, rope=None, block=0, blocks=1, earlier=None):
    rows, width = pre.shape
    tile = min(256, rows)
    tiles = rows // tile
    here = lambda i: (block * tiles + i, 0)
    operands = [pre, gains]
    in_specs = [
        pl.BlockSpec((tile, width), lambda i: (i, 0)),
        pl.BlockSpec((8, LANES), lambda i: (0, 0)),
    ]
    if rope is not None:
        operands.append(rope)
        in_specs.append(pl.BlockSpec((tile, 3 * LANES), here))
    for kind in kinds:
        if kind != "v":
            operands.append(extras[kind])
            in_specs.append(pl.BlockSpec((tile, LANES), here))
    aliases = {}
    if earlier is not None:
        for number, array in enumerate(earlier):
            aliases[len(operands)] = number
            operands.append(array)
            in_specs.append(pl.BlockSpec(memory_space=pl.ANY))
    out_shape = [
        jax.ShapeDtypeStruct((len(cols), blocks * rows, LANES), jnp.bfloat16) for cols in columns
    ]
    out_specs = [
        pl.BlockSpec((len(cols), tile, LANES), lambda i: (0, block * tiles + i, 0))
        for cols in columns
    ]
    heads = sum(len(cols) for cols in columns)
    return pl.pallas_call(
        functools.partial(
            cut_kernel,
            kinds=kinds,
            columns=columns,
            roped=rope is not None,
            chained=earlier is not None,
        ),
        grid=(tiles,),
        in_specs=in_specs,
        out_specs=out_specs,
        out_shape=out_shape,
        input_output_aliases=aliases,
        compiler_params=params("arbitrary"),
        cost_estimate=effort(heads * rows * 4.8e-4),
        name="cut_heads",
    )(*operands)


def join_kernel(*refs, kinds, columns, roped):
    pre_ref, gain_ref = refs[:2]
    place = 2
    if roped:
        rope_ref = refs[place]
        place += 1
    grads = refs[place : place + len(kinds)]
    out_ref, sum_ref = refs[place + len(kinds) :]
    part = min(256, pre_ref.shape[0])
    inside = lanes_of((part, LANES)) < HEAD_DIM

    @pl.when(pl.program_id(0) == 0)
    def _():
        sum_ref[...] = jnp.zeros_like(sum_ref)

    def rows_of(span):
        rope = rope_ref[span, :] if roped else None
        pieces = {}
        for number, kind in enumerate(kinds):
            total = jnp.zeros((part, LANES), jnp.float32)
            for head, offset in enumerate(columns[number]):
                slope = jnp.where(inside, grads[number][head, span, :], 0.0)
                if kind != "v":
                    slope = slope * (SCALE if kind == "q" else KEY_BACK)
                    if roped:
                        slope = turn_back(slope, rope)
                    values = pre_ref[span, offset : offset + HEAD_DIM].astype(jnp.float32)
                    normed, spread = head_norm(widen(values))
                    total = total + slope * normed
                    slope = slope * gain_ref[number : number + 1, :]
                    mean = lane_mean(slope, True)
                    mixed = lane_mean(slope * normed, False)
                    slope = (slope - mean - normed * mixed) * spread
                pieces[offset] = slope[:, :HEAD_DIM]
            if kind != "v":
                sum_ref[number : number + 1, :] += jnp.sum(total, 0, keepdims=True)
        out_ref[span, :] = jnp.concatenate(
            [pieces[offset] for offset in sorted(pieces)], 1
        ).astype(jnp.bfloat16)

    by_parts(pre_ref.shape[0], part, rows_of)


def join_heads(pre, gains, kinds, columns, grads, rope=None, block=0):
    rows, width = pre.shape
    tile = min(256, rows)
    tiles = rows // tile
    operands = [pre, gains]
    in_specs = [
        pl.BlockSpec((tile, width), lambda i: (i, 0)),
        pl.BlockSpec((8, LANES), lambda i: (0, 0)),
    ]
    if rope is not None:
        operands.append(rope)
        in_specs.append(pl.BlockSpec((tile, 3 * LANES), lambda i: (block * tiles + i, 0)))
    for array in grads:
        operands.append(array)
        in_specs.append(
            pl.BlockSpec((array.shape[0], tile, LANES), lambda i: (0, block * tiles + i, 0))
        )
    heads = sum(len(cols) for cols in columns)
    return pl.pallas_call(
        functools.partial(join_kernel, kinds=kinds, columns=columns, roped=rope is not None),
        grid=(tiles,),
        in_specs=in_specs,
        out_specs=[
            pl.BlockSpec((tile, width), lambda i: (i, 0)),
            pl.BlockSpec((8, LANES), lambda i: (0, 0)),
        ],
        out_shape=[
            jax.ShapeDtypeStruct((rows, width), jnp.bfloat16),
            jax.ShapeDtypeStruct((8, LANES), jnp.float32),
        ],
        compiler_params=params("arbitrary"),
        cost_estimate=effort(heads * rows * 9e-4),
        name="join_heads",
    )(*operands)


def attend_kernel(pick, q_ref, k_ref, v_ref, *refs, steps):
    o_ref, qx_ref = refs[-2:]
    step = pl.program_id(1)
    each, rows, _ = q_ref.shape
    part = min(256, rows)
    for start in range(0, rows, part):
        span = slice(start, start + part)
        merged = []
        for head in range(each):
            queries = q_ref[head, span, :]
            scores = lax.dot_general(
                queries, k_ref[head], ROW_TIMES_ROW, preferred_element_type=jnp.float32
            )
            weights = jnp.exp2(scores).astype(jnp.bfloat16)
            outputs = jnp.dot(weights, v_ref[head], preferred_element_type=jnp.float32)
            total = outputs[:, HEAD_DIM : HEAD_DIM + 1]
            merged.append((outputs * (1.0 / total))[:, :HEAD_DIM])
            level = -jnp.log2(total)
            high = level.astype(jnp.bfloat16).astype(jnp.float32)
            lane = lanes_of(outputs.shape)
            queries = queries.astype(jnp.float32)
            queries = jnp.where(lane == HEAD_DIM + 4, high, queries)
            queries = jnp.where(lane == HEAD_DIM + 5, level - high, queries)
            qx_ref[head, span, :] = queries.astype(jnp.bfloat16)
        merged = jnp.concatenate(merged, 1).astype(jnp.bfloat16)
        width = each * HEAD_DIM
        for number in range(steps):

            @pl.when(step == number)
            def _():
                o_ref[span, number * width : (number + 1) * width] = merged


def attend(queries, keys, values, pick, tile, key_rows, block=0, blocks=1, earlier=None):
    heads, rows_all, _ = queries.shape
    rows = rows_all // blocks
    tiles = rows // tile
    each = 2 if heads % 2 == 0 else 1
    there = lambda i, h, pick: (h, block * tiles + i, 0)
    keyed = lambda i, h, pick: (h, pick[i], 0)
    chained = [] if earlier is None else [earlier]
    return pl.pallas_call(
        functools.partial(attend_kernel, steps=heads // each),
        grid_spec=pltpu.PrefetchScalarGridSpec(
            num_scalar_prefetch=1,
            grid=(tiles, heads // each),
            in_specs=[
                pl.BlockSpec((each, tile, LANES), there),
                pl.BlockSpec((each, key_rows, LANES), keyed),
                pl.BlockSpec((each, key_rows, LANES), keyed),
            ]
            + [pl.BlockSpec(memory_space=pl.ANY)] * len(chained),
            out_specs=[
                pl.BlockSpec((tile, heads * HEAD_DIM), lambda i, h, pick: (i, 0)),
                pl.BlockSpec((each, tile, LANES), there),
            ],
        ),
        out_shape=[
            jax.ShapeDtypeStruct((rows, heads * HEAD_DIM), jnp.bfloat16),
            jax.ShapeDtypeStruct((heads, rows_all, LANES), jnp.bfloat16),
        ],
        input_output_aliases={4: 1} if chained else {},
        compiler_params=params("arbitrary", "arbitrary"),
        cost_estimate=effort(heads * rows * key_rows * 2.5e-6),
        name="attend",
    )(pick, queries, keys, values, *chained)


def cut_grad_kernel(*refs, heads):
    grad_ref, o_ref = refs[:2]
    out_ref = refs[-1]
    rows = grad_ref.shape[0]
    lane = lanes_of((rows, LANES))
    for head in range(heads):
        span = slice(head * HEAD_DIM, (head + 1) * HEAD_DIM)
        slope = grad_ref[:, span].astype(jnp.bfloat16).astype(jnp.float32)
        level = -jnp.sum(slope * o_ref[:, span].astype(jnp.float32), 1, keepdims=True)
        high = level.astype(jnp.bfloat16).astype(jnp.float32)
        slope = widen(slope)
        slope = jnp.where(lane == HEAD_DIM, high, slope)
        slope = jnp.where(lane == HEAD_DIM + 1, level - high, slope)
        out_ref[head] = slope.astype(jnp.bfloat16)


def cut_grad(grad, outputs, block=0, blocks=1, earlier=None):
    rows, width = grad.shape
    heads = width // HEAD_DIM
    tile = min(256, rows)
    tiles = rows // tile
    operands = [grad, outputs]
    in_specs = [pl.BlockSpec((tile, width), lambda i: (i, 0))] * 2
    aliases = {}
    if earlier is not None:
        aliases = {2: 0}
        operands.append(earlier)
        in_specs.append(pl.BlockSpec(memory_space=pl.ANY))
    return pl.pallas_call(
        functools.partial(cut_grad_kernel, heads=heads),
        grid=(tiles,),
        in_specs=in_specs,
        out_specs=pl.BlockSpec((heads, tile, LANES), lambda i: (0, block * tiles + i, 0)),
        out_shape=jax.ShapeDtypeStruct((heads, blocks * rows, LANES), jnp.bfloat16),
        input_output_aliases=aliases,
        compiler_params=params("arbitrary"),
        cost_estimate=effort(heads * rows * 6.5e-4),
        name="cut_grad",
    )(*operands)


def attend_back_kernel(pick, q_ref, k_ref, v_ref, g_ref, dq_ref, dk_ref, dv_ref, *, key_rows):
    tile = pl.program_id(1)
    queries, keys, slopes = q_ref[0], k_ref[0], g_ref[0]
    scores = lax.dot_general(keys, queries, ROW_TIMES_ROW, preferred_element_type=jnp.float32)
    weights = jnp.exp2(scores)
    pulls = lax.dot_general(v_ref[0], slopes, ROW_TIMES_ROW, preferred_element_type=jnp.float32)
    pulls = (weights * pulls).astype(jnp.bfloat16)
    value_grad = jnp.dot(weights.astype(jnp.bfloat16), slopes, preferred_element_type=jnp.float32)
    key_grad = jnp.dot(pulls, queries, preferred_element_type=jnp.float32)
    dq_ref[0] = lax.dot_general(pulls, keys, COL_TIMES_COL, preferred_element_type=jnp.float32)

    @pl.when(tile == 0)
    def _():
        dk_ref[...] = jnp.zeros_like(dk_ref)
        dv_ref[...] = jnp.zeros_like(dv_ref)

    start = pl.multiple_of(pick[tile] * key_rows, key_rows)
    dk_ref[0, pl.ds(start, key_rows), :] += key_grad
    dv_ref[0, pl.ds(start, key_rows), :] += value_grad


def attend_back(queries, keys, values, slopes, pick, tile, key_rows):
    heads, rows, _ = queries.shape
    all_keys = keys.shape[1]
    tiles = rows // tile
    there = lambda h, i, pick: (h, i, 0)
    keyed = lambda h, i, pick: (h, pick[i], 0)
    whole = lambda h, i, pick: (h, 0, 0)
    return pl.pallas_call(
        functools.partial(attend_back_kernel, key_rows=key_rows),
        grid_spec=pltpu.PrefetchScalarGridSpec(
            num_scalar_prefetch=1,
            grid=(heads, tiles),
            in_specs=[
                pl.BlockSpec((1, tile, LANES), there),
                pl.BlockSpec((1, key_rows, LANES), keyed),
                pl.BlockSpec((1, key_rows, LANES), keyed),
                pl.BlockSpec((1, tile, LANES), there),
            ],
            out_specs=[
                pl.BlockSpec((1, tile, LANES), there),
                pl.BlockSpec((1, all_keys, LANES), whole),
                pl.BlockSpec((1, all_keys, LANES), whole),
            ],
        ),
        out_shape=[
            jax.ShapeDtypeStruct((heads, rows, LANES), jnp.float32),
            jax.ShapeDtypeStruct((heads, all_keys, LANES), jnp.float32),
            jax.ShapeDtypeStruct((heads, all_keys, LANES), jnp.float32),
        ],
        compiler_params=params("arbitrary", "arbitrary"),
        cost_estimate=effort(heads * rows * key_rows * 3.5e-6),
        name="attend_back",
    )(pick, queries, keys, values, slopes)


def sum_product_kernel(*refs, blocks):
    lefts, rights, out_ref = refs[:blocks], refs[blocks : 2 * blocks], refs[-1]
    total = None
    for left, right in zip(lefts, rights):
        term = lax.dot_general(
            left[...], right[...], COL_TIMES_COL, preferred_element_type=jnp.float32
        )
        total = term if total is None else total + term
    out_ref[0] = total.astype(jnp.bfloat16)


def sum_product(lefts, rights, slot=0, slots=1, earlier=None):
    rows, depth = lefts[0].shape
    width = rights[0].shape[1]
    tile = min(512, width)
    blocks = len(lefts)
    chained = [] if earlier is None else [earlier]
    return pl.pallas_call(
        functools.partial(sum_product_kernel, blocks=blocks),
        grid=(pl.cdiv(width, tile),),
        in_specs=[pl.BlockSpec((rows, depth), lambda i: (0, 0))] * blocks
        + [pl.BlockSpec((rows, tile), lambda i: (0, i))] * blocks
        + [pl.BlockSpec(memory_space=pl.ANY)] * len(chained),
        out_specs=pl.BlockSpec((1, depth, tile), lambda i: (slot, 0, i)),
        out_shape=jax.ShapeDtypeStruct((slots, depth, width), jnp.bfloat16),
        input_output_aliases={2 * blocks: 0} if chained else {},
        compiler_params=params("arbitrary"),
        cost_estimate=effort(1 + 2 * blocks * rows * depth * width / 750e6),
        name="sum_product",
    )(*lefts, *rights, *chained)


def product_kernel(*refs, form):
    *terms, out_ref = refs
    half = len(terms) // 2
    total = None
    for left, right in zip(terms[:half], terms[half:]):
        term = lax.dot_general(
            left[...], right[...], form, preferred_element_type=jnp.float32
        )
        total = term if total is None else total + term
    out_ref[...] = total.astype(out_ref.dtype)


PLAIN = (((1,), (0,)), ((), ()))


def tile_of(width):
    for tile in (1024, 768, 1408, 512):
        if width % tile == 0:
            return tile
    return width if width < 1024 else 768


def right_spec(depth, tile, form):
    if form == PLAIN:
        return pl.BlockSpec((depth, tile), lambda i: (0, i))
    return pl.BlockSpec((tile, depth), lambda i: (i, 0))


def product(lefts, rights, form=PLAIN, kind=jnp.bfloat16):
    rows = lefts[0].shape[0]
    width = rights[0].shape[1 if form == PLAIN else 0]
    tile = tile_of(width)
    return pl.pallas_call(
        functools.partial(product_kernel, form=form),
        grid=(pl.cdiv(width, tile),),
        in_specs=[pl.BlockSpec(left.shape, lambda i: (0, 0)) for left in lefts]
        + [right_spec(left.shape[1], tile, form) for left in lefts],
        out_specs=pl.BlockSpec((rows, tile), lambda i: (0, i)),
        out_shape=jax.ShapeDtypeStruct((rows, width), kind),
        compiler_params=params("arbitrary"),
        cost_estimate=effort(1 + 2 * rows * width * sum(left.shape[1] for left in lefts) / 700e6),
        name="product",
    )(*lefts, *rights)


def gelu_kernel(rows_ref, weight_ref, slope_ref, active_ref, grad_ref):
    values = jnp.dot(rows_ref[...], weight_ref[...], preferred_element_type=jnp.float32)
    outer = 0.7978845608028654
    inner = 0.044715
    square = values * values
    bend = jnp.tanh(values * (outer + (outer * inner) * square))
    half = 0.5 + 0.5 * bend
    active_ref[...] = (values * half).astype(jnp.bfloat16)
    rise = (0.5 * outer + (1.5 * outer * inner) * square) * values
    slope = half + rise * (1.0 - bend * bend)
    grad_ref[...] = (slope_ref[...].astype(jnp.float32) * slope).astype(jnp.bfloat16)


def gelu_both(values, weight, slopes):
    rows, depth = values.shape
    width = weight.shape[1]
    tile = 512 if width % 512 == 0 else width
    return pl.pallas_call(
        gelu_kernel,
        grid=(width // tile,),
        in_specs=[
            pl.BlockSpec((rows, depth), lambda i: (0, 0)),
            pl.BlockSpec((depth, tile), lambda i: (0, i)),
            pl.BlockSpec((rows, tile), lambda i: (0, i)),
        ],
        out_specs=[pl.BlockSpec((rows, tile), lambda i: (0, i))] * 2,
        out_shape=[jax.ShapeDtypeStruct((rows, width), jnp.bfloat16)] * 2,
        compiler_params=params("arbitrary"),
        cost_estimate=effort(11),
        name="gelu_both",
    )(values, weight, slopes)


def row_mean(values):
    return jnp.mean(values, 1, keepdims=True)


def norm_rows(values):
    centre = values - row_mean(values)
    spread = lax.rsqrt(row_mean(centre * centre) + EPSILON)
    return centre * spread, spread


def norm_back(slope, normed, spread):
    return (slope - row_mean(slope) - normed * row_mean(slope * normed)) * spread


def sum_refs(refs):
    total = refs[0][...].astype(jnp.float32)
    for ref in refs[1:]:
        total = total + ref[...].astype(jnp.float32)
    return total


def add_gain_sum(ref, values, row=0):
    @pl.when(pl.program_id(0) == 0)
    def _():
        ref[row : row + 1, :] = jnp.zeros_like(ref[row : row + 1, :])

    ref[row : row + 1, :] += jnp.sum(values, 0, keepdims=True)


def first_norms_kernel(slots, hidden_ref, gains_ref, shifts_ref, residual_ref, normed_ref):
    slot = slots[pl.program_id(0)]
    normed, _ = norm_rows(hidden_ref[...])
    residual = normed * gains_ref[0:1, :]
    residual_ref[...] = residual
    again, _ = norm_rows(residual)
    shifted = again * gains_ref[1:2, :] + shifts_ref[pl.ds(slot, 1), :]
    normed_ref[...] = shifted.astype(jnp.bfloat16)


def add_norm_kernel(*refs):
    *terms, gain_ref, residual_ref, normed_ref = refs
    residual = sum_refs(terms)
    residual_ref[...] = residual
    normed, _ = norm_rows(residual)
    normed_ref[...] = (normed * gain_ref[0:1, :]).astype(jnp.bfloat16)


def norm_back_kernel(*refs):
    base_ref, residual_ref, *terms, gain_ref, grad_ref, low_ref, sum_ref = refs
    slope = sum_refs(terms)
    normed, spread = norm_rows(residual_ref[...])
    add_gain_sum(sum_ref, slope * normed)
    grad = base_ref[...].astype(jnp.float32)
    grad = grad + norm_back(slope * gain_ref[0:1, :], normed, spread)
    grad_ref[...] = grad
    low_ref[...] = grad.astype(jnp.bfloat16)


def first_norms_back_kernel(*refs):
    base_ref, hidden_ref, *terms, gains_ref, low_ref, sum_ref, slot_ref = refs
    slope = sum_refs(terms)
    normed, spread = norm_rows(hidden_ref[...])
    again, spread_again = norm_rows(normed * gains_ref[0:1, :])
    add_gain_sum(sum_ref, slope * again, 1)
    slot_ref[...] = jnp.broadcast_to(jnp.sum(slope, 0, keepdims=True), slot_ref.shape)
    slope = base_ref[...] + norm_back(slope * gains_ref[1:2, :], again, spread_again)
    add_gain_sum(sum_ref, slope * normed, 0)
    low_ref[...] = norm_back(slope * gains_ref[0:1, :], normed, spread).astype(jnp.bfloat16)


def row_call(kernel, name, tile, arrays, tables, outs, prefetch=None):
    rows, width = arrays[0].shape
    tiles = rows // tile
    scalars = [] if prefetch is None else [prefetch]
    by_tile = pl.BlockSpec((tile, width), lambda i, *_: (i, 0))
    out_specs, out_shape = [], []
    for out in outs:
        if out == "tile":
            out_specs.append(pl.BlockSpec((8, width), lambda i, *_: (i, 0)))
            out_shape.append(jax.ShapeDtypeStruct((8 * tiles, width), jnp.float32))
        elif isinstance(out, int):
            out_specs.append(pl.BlockSpec((out, width), lambda i, *_: (0, 0)))
            out_shape.append(jax.ShapeDtypeStruct((out, width), jnp.float32))
        else:
            out_specs.append(by_tile)
            out_shape.append(jax.ShapeDtypeStruct((rows, width), out))
    return pl.pallas_call(
        kernel,
        grid_spec=pltpu.PrefetchScalarGridSpec(
            num_scalar_prefetch=len(scalars),
            grid=(tiles,),
            in_specs=[by_tile] * len(arrays)
            + [pl.BlockSpec(table.shape, lambda i, *_: (0, 0)) for table in tables],
            out_specs=out_specs,
        ),
        out_shape=out_shape,
        compiler_params=params("arbitrary"),
        cost_estimate=effort(4),
        name=name,
    )(*scalars, *arrays, *tables)


def dot_rows(left, right):
    return lax.dot_general(left, right, ROW_TIMES_ROW, preferred_element_type=jnp.float32)


def dot_sum(left, right):
    return lax.dot_general(left, right, COL_TIMES_COL, preferred_element_type=jnp.float32)


def dot_plain(left, right):
    return jnp.dot(left, right, preferred_element_type=jnp.float32)


def low(values):
    return values.astype(jnp.bfloat16)


def wide(values):
    return values.astype(jnp.float32)


def after(values, *earlier):
    return lax.optimization_barrier((values,) + earlier)[0]


def from_back(values, step):
    size = lax.axis_size("seq")
    return lax.ppermute(values, "seq", [(i, (i + step) % size) for i in range(size)])


def to_back(values, step):
    size = lax.axis_size("seq")
    return lax.ppermute(values, "seq", [(i, (i - step) % size) for i in range(size)])


def gather_blocks(values):
    return [values] + [from_back(values, step) for step in range(1, lax.axis_size("seq"))]


def send_terms(terms):
    came = [to_back(terms[step], step) for step in range(1, len(terms))]
    if len(came) < 2:
        return came
    total = wide(came[0])
    for one in came[1:]:
        total = total + wide(one)
    return [total]


def row_spans(rows, *shares):
    edges, total = [0], 0
    for share in shares[:-1]:
        total += share
        edges.append(rows * total // sum(shares) // 16 * 16)
    edges.append(rows)
    return [(start, end) for start, end in zip(edges[:-1], edges[1:]) if end > start]


def sum_blocks(terms):
    total = wide(terms[0])
    for one in send_terms([None] + [low(term) for term in terms[1:]]):
        total = total + wide(one)
    return total


def swap_bit(values, axis, bit):
    size = lax.axis_size(axis)
    return lax.ppermute(values, axis, [(i, i ^ (1 << bit)) for i in range(size)])


def power_of_two(axis):
    size = lax.axis_size(axis)
    return size & (size - 1) == 0


def sum_over(values, axis):
    if not power_of_two(axis):
        return lax.psum(values, axis)
    for bit in range(lax.axis_size(axis).bit_length() - 1):
        values = values + swap_bit(values, axis, bit)
    return values


def unsigned(value):
    return value.astype(jnp.uint32)


def cut_at(values, start, size, axis):
    starts = [np.uint32(0)] * values.ndim
    starts[axis] = start
    sizes = list(values.shape)
    sizes[axis] = size
    return lax.dynamic_slice(values, starts, sizes)


def pick_at(values, index, axis):
    return lax.squeeze(cut_at(values, index, 1, axis), [axis])


class Places:
    def __init__(self, **numbers):
        names = list(numbers)
        leaves, tree = jax.tree.flatten([numbers[name] for name in names])
        self.all = lax.optimization_barrier(tuple(leaves))
        for name, value in zip(names, jax.tree.unflatten(tree, self.all)):
            setattr(self, name, value)


def bits_of(axis):
    place = lax.axis_index(axis)
    bits = [(place >> bit) & 1 for bit in range(lax.axis_size(axis).bit_length() - 1)]
    return [(unsigned(bit), unsigned(1 - bit), bit == 0) for bit in bits]


def gather_rows(values, axis, spot):
    if not power_of_two(axis):
        return lax.all_gather(values, axis, axis=0, tiled=True)
    for bit in range(lax.axis_size(axis).bit_length() - 1):
        came = swap_bit(values, axis, bit)
        values = jnp.where(
            spot.bits[bit][2],
            jnp.concatenate([values, came], 0),
            jnp.concatenate([came, values], 0),
        )
    return values


def gather_weight(half, earlier, hold, spot):
    size = lax.axis_size("seq")
    if size == 1:
        return []
    piece = pick_at(half.reshape(lax.axis_size("dp"), -1, half.shape[1]), spot.place, 0)
    pieces = [from_back(after(piece, *earlier), step) for step in range(1, size)]
    return [lax.all_gather(after(one, *hold), "dp", axis=0, tiled=True) for one in pieces]


def core_half(half, spot):
    return pick_at(half.reshape(2, -1, half.shape[1]), spot.bits[0][0], 0)


def join_halves(mine, other, spot):
    return jnp.where(
        spot.bits[0][2],
        jnp.concatenate([mine, other], 0),
        jnp.concatenate([other, mine], 0),
    )


class Summing:
    def __init__(self, grad, spot, high_first=False):
        self.parts = lax.axis_size("dp")
        self.top = self.parts.bit_length() - 2
        self.spot = spot
        self.groups, self.width = grad.shape[0], grad.shape[2]
        self.rows = grad.shape[1] // self.parts
        self.bits = list(range(1, self.top))
        if high_first:
            self.bits.reverse()
        self.left = list(range(self.top - 1, 0, -1))
        self.stage = -1
        self.grad = grad

    def split(self, held, axis, bit):
        mine, other, _ = self.spot.bits[bit]
        self.keep, self.sent = pick_at(held, mine, axis), pick_at(held, other, axis)

    def advance(self, *hold):
        if self.stage < 0:
            self.stage = 0
            grad = after(self.grad, *hold) if hold else self.grad
            self.split(grad.reshape(self.groups, 2, -1, self.width), 1, 0)
            self.came = swap_bit(self.sent, "dp", 0)
            return self
        held = self.keep + (after(self.came, *hold) if hold else self.came)
        if self.stage == 0:
            bits = (2,) * (self.top - 1)
            held = held.reshape((self.groups,) + bits + (2 * self.rows, self.width))
        self.stage += 1
        if self.bits:
            bit = self.bits.pop(0)
            axis = self.left.index(bit)
            self.left.remove(bit)
            self.split(held, axis + 1, bit)
            self.came = swap_bit(self.sent, "dp", bit)
        elif self.stage == self.top:
            senders = [i for i in range(self.parts) if (i >> self.top) != (i & 1)]
            self.keep = self.sent = held
            self.came = lax.ppermute(held, "dp", [(i, i ^ (1 << self.top)) for i in senders])
        else:
            owners = [i for i in range(self.parts) if (i >> self.top) == (i & 1)]
            self.split(held.reshape(self.groups, 2, self.rows, self.width), 1, 0)
            self.came = lax.ppermute(self.sent, "dp", [(i, i ^ 1) for i in owners])
        return self

    def finish(self, *hold):
        while self.stage <= self.top:
            self.advance(*hold)
            hold = ()
        came = after(self.came, *hold) if hold else self.came
        return wide(jnp.where(self.spot.owns, self.keep, came))


def advance_all(sums, *hold):
    for one in sums:
        one.advance(*hold)
        hold = (one.sent,)
    return hold[0]


def rope_table(rows, cols):
    quarter = HEAD_DIM // 4
    lane = jnp.arange(LANES, dtype=jnp.int32)
    rates = jnp.exp(
        -math.log(10000.0) * (lane % quarter).astype(jnp.float32) / quarter
    )
    angles = jnp.arange(SIDE, dtype=jnp.float32)[:, None] * rates[None, :]
    cosine, sine = jnp.cos(angles), jnp.sin(angles)
    leading = (lane // quarter) % 2 == 0
    table = jnp.concatenate(
        [cosine, jnp.where(leading, -sine, 0.0), jnp.where(leading, 0.0, sine)], 1
    )
    lane = jnp.tile(lane, 3)
    by_row = jnp.where(lane < HEAD_DIM // 2, table, 0.0)
    by_col = jnp.where((lane >= HEAD_DIM // 2) & (lane < HEAD_DIM), table, 0.0)
    spots = jnp.arange(SIDE, dtype=jnp.int32)[None, :]
    picks = jnp.concatenate([rows[:, None] == spots, cols[:, None] == spots], 1)
    return jnp.dot(
        picks.astype(jnp.float32), jnp.concatenate([by_row, by_col], 0), precision=PRECISE
    )


def extra_lanes(columns):
    lane = jnp.arange(LANES, dtype=jnp.int32)[None, :]
    table = jnp.zeros((columns[0].shape[0], LANES), jnp.float32)
    for number, column in enumerate(columns):
        table = jnp.where(lane == HEAD_DIM + number, column[:, None], table)
    return table


def gain_rows(*gains):
    stacked = jnp.stack(gains)
    return jnp.pad(stacked, ((0, 8 - len(gains)), (0, LANES - HEAD_DIM)))


def timestep_features(steps, width):
    halfway = width // 2
    rates = jnp.exp(-math.log(10000.0) * jnp.arange(halfway, dtype=jnp.float32) / halfway)
    angles = steps.astype(jnp.float32)[:, None] * rates[None, :]
    return jnp.concatenate([jnp.cos(angles), jnp.sin(angles)], 1)


def on_device(
    latent,
    skip_input,
    clip_text,
    t5_text,
    bucket,
    counts,
    language,
    timesteps,
    cotangent,
    skip_weight,
    skip_gain,
    time_weight,
    shift_weight,
    norm1_gain,
    qkv_weight,
    q_gain,
    k_gain,
    out_weight,
    norm3_gain,
    cross_query,
    cq_gain,
    t5_weight,
    lang_embed,
    cross_kv,
    ck_gain,
    cross_out,
    norm2_gain,
    fc1_weight,
    fc2_weight,
):
    size = lax.axis_size("seq")
    me = lax.axis_index("seq")
    place = lax.axis_index("dp")
    parts = lax.axis_size("dp")
    rows, width = latent.shape
    local_width = out_weight.shape[0]
    local_heads = local_width // HEAD_DIM
    all_heads = local_heads * size
    clip_length, text_local = clip_text.shape[1:]
    text_length = t5_text.shape[1]
    text_width = lang_embed.shape[1]
    tokens = rows * size
    small = (bucket[0] == 1).astype(jnp.int32)
    quarter = tokens // SMALL_PER
    tile = min(quarter, rows)
    slots = max(1, rows // quarter)

    def owner(step):
        return (me - step) % size

    def first_slot(device):
        return small * (device * rows // quarter)

    def slot_places(device):
        found = []
        for slot in range(SMALL_PER):
            offset = slot - first_slot(device)
            inside = (offset >= 0) & (offset < slots)
            found.append((wide(inside), unsigned(jnp.clip(offset, 0, slots - 1))))
        return found

    owners = [owner(step) for step in range(size)]
    ahead = [(me + step) % size for step in range(size)]
    top = parts.bit_length() - 2
    spot = Places(
        place=unsigned(place),
        place_slots=unsigned(place * SMALL_PER),
        place_columns=unsigned(place * (width // parts)),
        bits=bits_of("dp"),
        owns=(place >> top) == (place & 1),
        first=me == 0,
        me_columns=unsigned(me * local_width),
        text_spans=[unsigned(device * text_local) for device in owners],
        joined_spans=[unsigned(device * (2 * width // size)) for device in owners],
        joined_ahead=[unsigned(device * (2 * width // size)) for device in ahead],
        sides=[
            unsigned(side * (width // size)) for side in ((place & 1), 1 - (place & 1))
        ],
        slots_back=[unsigned(first_slot(device)) for device in owners],
        slots_ahead=[unsigned(first_slot(device)) for device in ahead],
        spread=[slot_places(device) for device in ahead],
    )

    order = jnp.concatenate(
        [owner(step) * rows + jnp.arange(rows, dtype=jnp.int32) for step in range(size)]
    )
    slot_of = jnp.where(small == 1, order // quarter, 0)
    within = jnp.where(small == 1, order % quarter, order)
    across = jnp.where(small == 1, SIDE // 2, SIDE)
    rope = rope_table(within // across, within % across)
    own_slots = slot_of[:rows]
    self_extras = dict(
        q=extra_lanes([wide(slot_of == j) for j in range(SMALL_PER)]),
        k=extra_lanes(
            [jnp.where(slot_of == j, 0.0, HIDE) for j in range(SMALL_PER)]
            + [jnp.ones((tokens,), jnp.float32)] * 2
        ),
    )

    qkv_rows = qkv_weight.transpose(1, 2, 0).reshape(3 * local_width, width)
    cq_own = cross_query.T
    kv_own = cross_kv.transpose(1, 2, 0).reshape(2 * local_width, text_width)
    skip_piece = core_half(skip_weight, spot)
    skip_pieces = [from_back(skip_piece, step) for step in range(1, size)]
    active_slopes = [product([cotangent], [fc2_weight], ROW_TIMES_ROW)]
    timesteps = after(timesteps, skip_piece)
    tile_slots = own_slots[::tile]
    slot_masks = wide(tile_slots[:, None] == jnp.arange(SMALL_PER, dtype=jnp.int32)[None, :])
    first_gains = jnp.stack([skip_gain, norm1_gain])
    self_gains = gain_rows(q_gain, k_gain)
    kv_gains = gain_rows(ck_gain, ck_gain)
    query_gains = gain_rows(cq_gain)
    third_gain, second_gain = norm3_gain[None, :], norm2_gain[None, :]
    cross_pick = small * (jnp.arange(rows // tile, dtype=jnp.int32) * tile // quarter)

    my_languages = cut_at(language, spot.slots_back[0], slots, 0)
    words = wide(lang_embed)
    chosen = jnp.where((my_languages == 1)[:, None], words[1][None, :], words[0][None, :])
    my_counts = cut_at(counts, spot.slots_back[0], slots, 0)
    key_place = jnp.arange(KEY_ROWS, dtype=jnp.int32)[None, :]
    visible = jnp.where(
        key_place < text_length,
        key_place < my_counts[:, 1:],
        (key_place - text_length < my_counts[:, :1]) & (key_place < text_length + clip_length),
    ).reshape(-1)
    cross_key_extra = jnp.where(visible, 0.0, HIDE)
    ones_keys = jnp.ones((slots * KEY_ROWS,), jnp.float32)
    zeros_keys = jnp.zeros((slots * KEY_ROWS,), jnp.float32)
    cross_extras = dict(
        q=extra_lanes([jnp.ones((rows,), jnp.float32)]),
        k=extra_lanes([cross_key_extra, zeros_keys, zeros_keys, zeros_keys, ones_keys, ones_keys]),
    )
    tables = [
        *spot.all,
        tile_slots,
        slot_masks,
        first_gains,
        self_gains,
        kv_gains,
        query_gains,
        third_gain,
        second_gain,
        cross_pick,
        chosen,
        *cross_extras.values(),
        *self_extras.values(),
        rope,
    ]

    steps_all = gather_rows(timesteps, "dp", spot)
    features_all = low(timestep_features(steps_all, time_weight.shape[0]))
    gate_all, silu_pull = jax.vjp(jax.nn.silu, dot_plain(features_all, time_weight))
    gate_all = low(gate_all)
    gate = cut_at(gate_all, spot.place_slots, SMALL_PER, 0)
    shift_own = low(dot_plain(gate, shift_weight))
    shift_blocks = gather_blocks(shift_own)
    if size == 2:
        shifts = jnp.where(
            spot.first,
            jnp.concatenate(shift_blocks, 1),
            jnp.concatenate(shift_blocks[::-1], 1),
        )
    else:
        shifts = lax.all_gather(shift_own, "seq", axis=1, tiled=True)

    partial = product([t5_text.reshape(-1, t5_text.shape[2])], [t5_weight])
    partial = partial.reshape(SMALL_PER, text_length, text_width)
    if size == 2:
        chunk = [
            jnp.where(spot.first, latent, skip_input),
            jnp.where(spot.first, skip_input, latent),
        ]
    else:
        joined = jnp.concatenate([latent, skip_input], 1)
        part = 2 * width // size
        chunk = [
            cut_at(joined, spot.joined_spans[step], part, 1) for step in range(size)
        ]
    half_depth = chunk[0].shape[1] // 2
    lefts, rights = [chunk[0]], [skip_weight]
    for step in range(1, size):
        lefts += [cut_at(chunk[step], side, half_depth, 1) for side in spot.sides]
    skip_pieces = [after(block, partial, shifts, active_slopes[0], *tables, *lefts) for block in skip_pieces]
    skip_others = [swap_bit(piece, "dp", 0) for piece in skip_pieces]
    for mine, other in zip(skip_pieces, skip_others):
        rights += [mine, other]
    spare = width - text_width
    cross_rows = jnp.concatenate([cq_own, cross_out, jnp.pad(kv_own, ((0, 0), (0, spare)))], 0)
    cross_blocks = [cross_rows] + gather_weight(cross_rows, skip_pieces, skip_others, spot)
    cq_full = jnp.concatenate([block[:local_width] for block in cross_blocks], 0)
    co_full = jnp.concatenate(
        [block[local_width : 2 * local_width] for block in cross_blocks], 0
    )
    kv_full = jnp.concatenate(
        [block[2 * local_width :, :text_width] for block in cross_blocks], 0
    )


    text_terms = [cut_at(partial, spot.slots_back[step], slots, 0) for step in range(size)]
    text_came = send_terms([after(term, *skip_pieces) for term in text_terms])
    clip_came = []
    for step in range(size):
        block = cut_at(after(clip_text, *skip_pieces), spot.slots_ahead[step], slots, 0)
        clip_came.append(from_back(block, step) if step else block)

    hidden = product(lefts, rights, kind=jnp.float32)
    residual_one, normed = row_call(
        first_norms_kernel,
        "first_norms",
        tile,
        [hidden],
        [first_gains, wide(shifts)],
        [jnp.float32, jnp.bfloat16],
        tile_slots,
    )
    normed_blocks = gather_blocks(normed)


    self_kinds = ("q", "k", "v")
    self_columns = [
        [local_width * which + HEAD_DIM * head for head in range(local_heads)]
        for which in range(3)
    ]
    qkv_blocks, cut = [], None
    for step in range(size):
        qkv_blocks.append(product([normed_blocks[step]], [qkv_rows], ROW_TIMES_ROW))
        if step == 0 and size > 1:
            normed_blocks[1] = after(normed_blocks[1], qkv_blocks[0])
        cut = cut_heads(
            qkv_blocks[step],
            self_gains,
            self_kinds,
            self_columns,
            self_extras,
            rope,
            step,
            size,
            cut,
        )
    queries, keys, values = cut
    no_pick = jnp.zeros((1,), jnp.int32)
    self_outputs, self_queries = [None] * size, None
    out_terms = [None] * size
    for step in list(range(1, size)) + [0]:
        if step == 0:
            queries = after(queries, *out_terms[1:])
        self_outputs[step], self_queries = attend(
            queries, keys, values, no_pick, rows, tokens, step, size, self_queries
        )
        out_terms[step] = product([self_outputs[step]], [out_weight])
    out_came = send_terms(out_terms)

    hold = out_terms[1:] + text_came + clip_came[1:]
    text_came = [after(came, *hold) for came in text_came]
    clip_came = [after(came, *hold) for came in clip_came]
    projected = wide(text_terms[0])
    for came in text_came:
        projected = projected + wide(came)
    clip_full = jnp.zeros((slots, clip_length, text_width), jnp.bfloat16)
    zero = np.uint32(0)
    for block, span in zip(clip_came, spot.text_spans):
        clip_full = lax.dynamic_update_slice(clip_full, block, [zero, zero, span])
    unused = KEY_ROWS - text_length - clip_length
    context = jnp.concatenate(
        [
            low(projected + chosen[:, None, :]),
            clip_full,
            jnp.zeros((slots, unused, text_width), jnp.bfloat16),
        ],
        1,
    ).reshape(slots * KEY_ROWS, text_width)
    context_kv = product([context], [kv_full], ROW_TIMES_ROW)
    key_columns = [
        2 * local_width * group + HEAD_DIM * head
        for group in range(size)
        for head in range(local_heads)
    ]
    kv_columns = [key_columns, [column + local_width for column in key_columns]]
    cross_keys, cross_values = cut_heads(
        context_kv, kv_gains, ("k", "v"), kv_columns, cross_extras
    )

    out_came = [after(came, out_terms[0], cross_keys) for came in out_came]
    cotangent_blocks = gather_blocks(after(cotangent, *out_came))
    residual_two, normed_cross = row_call(
        add_norm_kernel,
        "cross_norm",
        tile,
        [residual_one, out_terms[0], *out_came],
        [third_gain],
        [jnp.float32, jnp.bfloat16],
    )

    cross_pre = product([normed_cross], [cq_full], ROW_TIMES_ROW)
    query_columns = [[HEAD_DIM * head for head in range(all_heads)]]
    (cross_queries,) = cut_heads(cross_pre, query_gains, ("q",), query_columns, cross_extras)
    cross_outputs, cross_queries = attend(
        cross_queries, cross_keys, cross_values, cross_pick, tile, KEY_ROWS
    )
    residual_three, normed_mlp = row_call(
        add_norm_kernel,
        "mlp_norm",
        tile,
        [residual_two, product([cross_outputs], [co_full])],
        [second_gain],
        [jnp.float32, jnp.bfloat16],
    )

    mlp_blocks = gather_blocks(normed_mlp)
    active, expanded_grads, mlp_terms = [], [], []
    for step in range(size):
        gate_out, gate_grad = gelu_both(mlp_blocks[step], fc1_weight, active_slopes[step])
        active.append(gate_out)
        expanded_grads.append(gate_grad)
        mlp_terms.append(product([gate_grad], [fc1_weight], ROW_TIMES_ROW))
        if step == 0:
            fc_terms = [product([active[0]], [fc2_weight])]
            active_slopes += [
                product([block], [fc2_weight], ROW_TIMES_ROW) for block in cotangent_blocks[1:]
            ]
            mlp_blocks[1:] = [
                after(block, mlp_terms[0], fc_terms[0], *active_slopes[1:])
                for block in mlp_blocks[1:]
            ]
    mlp_came = send_terms(mlp_terms)
    fc_sum = sum_product([after(one, *mlp_terms[1:]) for one in cotangent_blocks], active, 0, 2)
    fc_sum = sum_product(mlp_blocks, expanded_grads, 1, 2, fc_sum)
    for step in range(1, size):
        fc_terms.append(product([after(active[step], fc_sum)], [fc2_weight]))
    mlp_came = [after(came, fc_sum, *fc_terms) for came in mlp_came]
    fc_sums = [Summing(fc_sum, spot)]
    fc_terms[1:] = [after(term, *mlp_came) for term in fc_terms[1:]]
    fc_came = send_terms(fc_terms)

    sent = advance_all(fc_sums, *mlp_came)
    mlp_came = [after(came, sent) for came in mlp_came]
    grad_three, three_low, norm2_sum = row_call(
        norm_back_kernel,
        "mlp_norm_back",
        tile,
        [cotangent, residual_three, mlp_terms[0], *mlp_came],
        [second_gain],
        [jnp.float32, jnp.bfloat16, 8],
    )

    cross_slopes = cut_grad(product([three_low], [co_full], ROW_TIMES_ROW), cross_outputs)
    cross_slopes = after(cross_slopes, advance_all(fc_sums, cross_slopes))
    grad_cq, grad_ck, grad_cv = attend_back(
        cross_queries, cross_keys, cross_values, cross_slopes, cross_pick, tile, KEY_ROWS
    )
    fc_came = [after(came, grad_cq) for came in fc_came]
    block_output = residual_three + wide(fc_terms[0])
    for came in fc_came:
        block_output = block_output + wide(came)
    block_output = low(block_output)
    joined_blocks = [chunk[0]]
    for step in range(1, size):
        if size == 2:
            block = chunk[1]
        else:
            block = cut_at(joined, spot.joined_ahead[step], part, 1)
        block = after(block, *fc_terms)
        joined_blocks.append(from_back(block, step))
    grad_cq = after(grad_cq, block_output)
    cross_pre_grad, query_sums = join_heads(
        cross_pre, query_gains, ("q",), query_columns, (grad_cq,)
    )
    cross_slope = product([cross_pre_grad], [cq_full])
    cross_slope = after(cross_slope, *joined_blocks[1:])
    grad_two, two_low, norm3_sum = row_call(
        norm_back_kernel,
        "cross_norm_back",
        tile,
        [grad_three, residual_two, cross_slope],
        [third_gain],
        [jnp.float32, jnp.bfloat16, 8],
    )
    two_blocks = gather_blocks(two_low)
    context_kv_grad, key_sums = join_heads(
        context_kv, kv_gains, ("k", "v"), kv_columns, (after(grad_ck, two_low), grad_cv)
    )
    kv_sum = sum_product([context], [context_kv_grad])
    context_grad = product([context_kv_grad], [kv_full], kind=jnp.float32)
    context_grad = context_grad.reshape(slots, KEY_ROWS, text_width)

    def own_part(summed):
        blocks = [
            summed[:, step * (summed.shape[1] // size) : (step + 1) * (summed.shape[1] // size)]
            for step in range(size)
        ]
        return sum_blocks(blocks)

    later = after(three_low, two_low)
    cross_sum = sum_product([later], [cross_outputs], 0, 2)
    cross_sum = sum_product([normed_cross], [cross_pre_grad], 1, 2, cross_sum)
    two_blocks[1:] = [
        after(block, cross_sum, kv_sum, context_grad) for block in two_blocks[1:]
    ]
    cross_sums = [Summing(kv_sum, spot), Summing(cross_sum, spot)]
    sent = advance_all(fc_sums + cross_sums, *two_blocks[1:])
    two_blocks[1:] = [after(block, sent) for block in two_blocks[1:]]

    def spread_slots(blocks):
        found = []
        for slot in range(SMALL_PER):
            total = 0.0
            for step, block in enumerate(blocks):
                inside, index = spot.spread[step][slot]
                total = total + inside * wide(pick_at(block, index, 0))
            found.append(total)
        return jnp.stack(found)

    text_grad = context_grad[:, :text_length]
    text_low = after(low(text_grad), *two_blocks[1:])
    text_blocks = [text_low] + [to_back(text_low, step) for step in range(1, size)]
    clip_blocks = []
    for step in range(size):
        block = cut_at(
            context_grad[:, text_length : text_length + clip_length],
            spot.text_spans[step],
            text_local,
            2,
        )
        clip_blocks.append(to_back(after(low(block), text_low), step) if step else block)
    slopes = None
    for step in range(size):
        slopes = cut_grad(
            product([two_blocks[step]], [out_weight], ROW_TIMES_ROW), self_outputs[step], step, size, slopes
        )
    slopes = after(slopes, advance_all(cross_sums, slopes))
    back_tile = min(512, tokens)
    head_grads = attend_back(
        self_queries,
        keys,
        values,
        slopes,
        jnp.zeros((tokens // back_tile,), jnp.int32),
        back_tile,
        tokens,
    )
    sent = advance_all(fc_sums, head_grads[0])
    head_grads = [
        after(head_grads[0], sent, *text_blocks[1:], *clip_blocks[1:]),
        *head_grads[1:],
    ]
    qkv_grads, normed_terms = [None] * size, [None] * size
    self_sums = 0.0
    for step in list(range(1, size)) + [0]:
        if step == 0:
            head_grads = [after(head_grads[0], *normed_terms[1:]), *head_grads[1:]]
        qkv_grads[step], sums = join_heads(
            qkv_blocks[step], self_gains, self_kinds, self_columns, head_grads, rope, step
        )
        self_sums = self_sums + sums
        normed_terms[step] = product([qkv_grads[step]], [qkv_rows])
    normed_came = send_terms(normed_terms)
    qkv_sum = sum_product(normed_blocks, qkv_grads)
    normed_terms[0] = after(normed_terms[0], qkv_sum)
    normed_came = [after(came, normed_terms[0]) for came in normed_came]
    qkv_sums = [Summing(qkv_sum, spot)]
    sent = advance_all(qkv_sums, *normed_came)
    normed_came = [after(came, sent) for came in normed_came]

    hidden_low, first_sums, slot_sums = row_call(
        first_norms_back_kernel,
        "first_norms_back",
        tile,
        [grad_two, hidden, normed_terms[0], *normed_came],
        [first_gains],
        [jnp.bfloat16, 8, "tile"],
    )
    hidden_blocks = gather_blocks(hidden_low)
    sent = advance_all(qkv_sums + fc_sums + cross_sums, hidden_low)
    out_sum = sum_product(after(two_blocks, sent), self_outputs)
    text_blocks[0] = after(text_blocks[0], out_sum)
    project_all = low(spread_slots(text_blocks)).reshape(SMALL_PER * text_length, text_width)
    t5_sum = sum_product([project_all], [t5_text.reshape(-1, t5_text.shape[2])])
    out_sums, t5_sums = [Summing(out_sum, spot)], [Summing(t5_sum, spot, True)]
    hidden_blocks[1:] = [after(block, t5_sum) for block in hidden_blocks[1:]]
    skip_sum = sum_product(hidden_blocks, joined_blocks)
    skip_sums = [Summing(skip_sum, spot)]
    sent = advance_all(skip_sums + out_sums + t5_sums + cross_sums + qkv_sums, skip_sum)
    sent = advance_all(skip_sums + out_sums + t5_sums, sent)

    tongues = wide(my_languages[None, :] == jnp.arange(2, dtype=jnp.int32)[:, None])
    grad_lang = jnp.dot(tongues, jnp.sum(text_grad, 1), precision=PRECISE)
    gains = [
        first_sums[0],
        first_sums[1],
        self_sums[0, :HEAD_DIM],
        self_sums[1, :HEAD_DIM],
        norm3_sum[0],
        query_sums[0, :HEAD_DIM],
        key_sums[0, :HEAD_DIM],
        norm2_sum[0],
        grad_lang.reshape(-1),
    ]
    packed = after(jnp.concatenate(gains), t5_sum)
    packed_came = swap_bit(packed, "dp", 0)
    shift_terms = jnp.zeros((SMALL_PER, width), jnp.float32)
    for number in range(rows // tile):
        shift_terms += slot_masks[number][:, None] * after(slot_sums, t5_sum)[8 * number][None, :]
    shift_sum = sum_over(shift_terms, "seq")
    hidden_low = after(hidden_low, sent)
    skip_blocks = [skip_weight]
    for mine, other in zip(skip_pieces, skip_others):
        skip_blocks.append(join_halves(mine, after(other, sent), spot))
    joined_grads = [
        product([hidden_low], [block], ROW_TIMES_ROW, jnp.float32) for block in skip_blocks
    ]
    fc_total = fc_sums[0].finish(*joined_grads)
    grad_fc2, grad_fc1 = fc_total[0].T, fc_total[1]
    sent = advance_all(qkv_sums + skip_sums + cross_sums, fc_total)
    packed = packed + after(packed_came, sent)
    shift_low = low(after(shift_sum, sent))
    project_all = after(project_all, packed, shift_low)
    grad_t5 = product([project_all], [t5_weight], ROW_TIMES_ROW, jnp.float32)
    grad_t5 = grad_t5.reshape(t5_text.shape)
    sent = advance_all(out_sums + t5_sums + skip_sums + qkv_sums, grad_t5)
    sent = advance_all(out_sums + t5_sums, sent)
    clip_blocks[0] = after(clip_blocks[0], sent)
    grad_clip = spread_slots(clip_blocks)
    if size == 2:
        grad_latent = jnp.where(spot.first, joined_grads[0], joined_grads[1])
        grad_skip_input = jnp.where(spot.first, joined_grads[1], joined_grads[0])
    else:
        joined_grad = jnp.zeros((rows, 2 * width), jnp.float32)
        for step in range(size):
            joined_grad = lax.dynamic_update_slice(
                joined_grad, joined_grads[step], [np.uint32(0), spot.joined_spans[step]]
            )
        grad_latent, grad_skip_input = joined_grad[:, :width], joined_grad[:, width:]

    shift_all = gather_rows(shift_low, "dp", spot)
    shift_mine = cut_at(shift_all, spot.me_columns, local_width, 1)
    gate_mine = cut_at(gate_all, spot.place_columns, width // parts, 1)
    grad_shift = dot_sum(gate_mine, shift_mine)
    (time_slope,) = silu_pull(sum_over(dot_rows(shift_mine, shift_weight), "seq"))
    grad_time = jnp.dot(wide(features_all).T, time_slope, precision=PRECISE)

    grad_skip_weight = skip_sums[0].finish()[0].T
    grad_qkv = qkv_sums[0].finish().reshape(-1, 3, local_width)
    grad_out = out_sums[0].finish()[0].T
    grad_t5_weight = t5_sums[0].finish()[0].T
    kv_total, cross_total = [one.finish() for one in cross_sums]
    grad_cross_kv = own_part(kv_total[0]).reshape(-1, 2, local_width)
    grad_cross_out = own_part(cross_total[0]).T
    grad_cross_query = own_part(cross_total[1])

    for bit in range(1, lax.axis_size("dp").bit_length() - 1):
        packed = packed + swap_bit(packed, "dp", bit)
    packed = sum_over(packed, "seq")
    totals, start = [], 0
    for gain in gains:
        totals.append(packed[start : start + gain.shape[0]])
        start += gain.shape[0]
    return (
        block_output,
        grad_latent,
        grad_skip_input,
        grad_clip,
        grad_t5,
        grad_skip_weight,
        totals[0],
        grad_time,
        grad_shift,
        totals[1],
        grad_qkv,
        totals[2],
        totals[3],
        grad_out,
        totals[4],
        grad_cross_query,
        totals[5],
        grad_t5_weight,
        totals[8].reshape(lang_embed.shape),
        grad_cross_kv,
        totals[6],
        grad_cross_out,
        totals[7],
        grad_fc1,
        grad_fc2,
    )


def solution(mesh):
    return jax.shard_map(
        on_device,
        mesh=mesh,
        in_specs=(
            P(("dp", "seq"), None),
            P(("dp", "seq"), None),
            P("dp", None, "seq"),
            P("dp", None, "seq"),
            P("dp"),
            P("dp", None),
            P("dp"),
            P("dp"),
            P(("dp", "seq"), None),
            P("seq", None),
            P(),
            P(),
            P(None, "seq"),
            P(),
            P(None, None, "seq"),
            P(),
            P(),
            P("seq", None),
            P(),
            P(None, "seq"),
            P(),
            P("seq", None),
            P(),
            P(None, None, "seq"),
            P(),
            P("seq", None),
            P(),
            P(None, "seq"),
            P("seq", None),
        ),
        out_specs=(
            P(("dp", "seq"), None),
            P(("dp", "seq"), None),
            P(("dp", "seq"), None),
            P("dp", None, "seq"),
            P("dp", None, "seq"),
            P("seq", "dp"),
            P(),
            P(),
            P("dp", "seq"),
            P(),
            P("dp", None, "seq"),
            P(),
            P(),
            P("seq", "dp"),
            P(),
            P("dp", "seq"),
            P(),
            P("seq", "dp"),
            P(),
            P("dp", None, "seq"),
            P(),
            P("seq", "dp"),
            P(),
            P("dp", "seq"),
            P("seq", "dp"),
        ),
        check_vma=False,
    )
```

```python
import copy
import functools
import math

import jax
import jax.numpy as jnp
import numpy as np
from jax import lax
from jax.experimental import pallas as pl
from jax.experimental.pallas import tpu as pltpu
from jax.sharding import PartitionSpec as P

HEAD_DIM = 88
SIDE = 32
SMALL_PER = 4
LANES = 128
KEY_ROWS = 384

PRECISE = lax.Precision.HIGHEST
EPSILON = 1e-06
HIDE = -30000.0
SCALE = 1.0 / math.sqrt(HEAD_DIM)
QUERY_SCALE = SCALE * math.log2(math.e)
KEY_BACK = math.log(2.0)
VMEM = 20 * 1024 * 1024


SCALE_FLOPS = 2e8
EACH_BACK = 2


def effort(us):
    return pl.CostEstimate(flops=int(us * SCALE_FLOPS), bytes_accessed=1, transcendentals=0)


ROW_TIMES_ROW = (((1,), (1,)), ((), ()))
COL_TIMES_COL = (((0,), (0,)), ((), ()))


def params(*semantics):
    return pltpu.CompilerParams(dimension_semantics=semantics, vmem_limit_bytes=VMEM)


def lanes_of(shape):
    return lax.broadcasted_iota(jnp.int32, shape, len(shape) - 1)


def widen(values):
    fill = jnp.zeros((values.shape[0], LANES - HEAD_DIM), values.dtype)
    return jnp.concatenate([values, fill], 1)


def lane_mean(values, exact):
    high = values.astype(jnp.bfloat16)
    if exact:
        low = (values - high.astype(jnp.float32)).astype(jnp.bfloat16)
        high = jnp.concatenate([high, low], 1)
    ones = jnp.full((high.shape[1], LANES), 1.0, jnp.bfloat16)
    return jnp.dot(high, ones, preferred_element_type=jnp.float32) * (1.0 / HEAD_DIM)


def head_norm(values):
    inside = lanes_of(values.shape) < HEAD_DIM
    centre = jnp.where(inside, values - lane_mean(values, True), 0.0)
    spread = lax.rsqrt(lane_mean(centre * centre, False) + EPSILON)
    return centre * spread, spread


def by_parts(ref_rows, part, body):
    def step(number, carry):
        body(pl.ds(pl.multiple_of(number * part, part), part))
        return carry

    lax.fori_loop(0, ref_rows // part, step, 0)


def turn(values, rope):
    cosine, lead, trail = rope[:, :LANES], rope[:, LANES : 2 * LANES], rope[:, 2 * LANES :]
    quarter = HEAD_DIM // 4
    ahead = pltpu.roll(values, LANES - quarter, 1)
    behind = pltpu.roll(values, quarter, 1)
    return values * cosine + ahead * lead + behind * trail


def turn_back(values, rope):
    cosine, lead, trail = rope[:, :LANES], rope[:, LANES : 2 * LANES], rope[:, 2 * LANES :]
    quarter = HEAD_DIM // 4
    ahead = pltpu.roll(values, LANES - quarter, 1)
    behind = pltpu.roll(values, quarter, 1)
    return values * cosine - ahead * lead - behind * trail


def cut_kernel(*refs, kinds, columns, roped, chained):
    pre_ref, gain_ref = refs[:2]
    place = 2
    if roped:
        rope_ref = refs[place]
        place += 1
    extras = {}
    for kind in kinds:
        if kind != "v":
            extras[kind] = refs[place]
            place += 1
    normed_kinds = [number for number, kind in enumerate(kinds) if kind != "v"]
    if chained:
        place += len(kinds) + len(normed_kinds)
    outs = refs[place : place + len(kinds)]
    keeps = dict(zip(normed_kinds, refs[place + len(kinds) :]))
    part = min(64, pre_ref.shape[0])
    lane = lanes_of((part, LANES))
    ones = jnp.where((lane == HEAD_DIM) | (lane == HEAD_DIM + 1), 1.0, 0.0)

    def rows_of(span):
        rope = rope_ref[span, :] if roped else None
        for number, kind in enumerate(kinds):
            for head, offset in enumerate(columns[number]):
                values = pre_ref[span, offset : offset + HEAD_DIM].astype(jnp.float32)
                values = widen(values)
                if kind == "v":
                    outs[number][head, span, :] = (values + ones).astype(jnp.bfloat16)
                    continue
                normed, spread = head_norm(values)
                high = spread.astype(jnp.bfloat16).astype(jnp.float32)
                kept = jnp.where(lane == HEAD_DIM, high, normed)
                kept = jnp.where(lane == HEAD_DIM + 1, spread - high, kept)
                keeps[number][head, span, :] = kept.astype(jnp.bfloat16)
                normed = normed * gain_ref[number : number + 1, :]
                if roped:
                    normed = turn(normed, rope)
                if kind == "q":
                    normed = normed * QUERY_SCALE
                outs[number][head, span, :] = (normed + extras[kind][span, :]).astype(jnp.bfloat16)

    by_parts(pre_ref.shape[0], part, rows_of)


def cut_heads(pre, gains, kinds, columns, extras, rope=None, block=0, blocks=1, earlier=None):
    rows, width = pre.shape
    tile = min(256, rows)
    tiles = rows // tile
    here = lambda i: (block * tiles + i, 0)
    operands = [pre, gains]
    in_specs = [
        pl.BlockSpec((tile, width), lambda i: (i, 0)),
        pl.BlockSpec((8, LANES), lambda i: (0, 0)),
    ]
    if rope is not None:
        operands.append(rope)
        in_specs.append(pl.BlockSpec((tile, 3 * LANES), here))
    for kind in kinds:
        if kind != "v":
            operands.append(extras[kind])
            in_specs.append(pl.BlockSpec((tile, LANES), here))
    aliases = {}
    if earlier is not None:
        for number, array in enumerate(earlier):
            aliases[len(operands)] = number
            operands.append(array)
            in_specs.append(pl.BlockSpec(memory_space=pl.ANY))
    out_columns = columns + [cols for kind, cols in zip(kinds, columns) if kind != "v"]
    out_shape = [
        jax.ShapeDtypeStruct((len(cols), blocks * rows, LANES), jnp.bfloat16)
        for cols in out_columns
    ]
    out_specs = [
        pl.BlockSpec((len(cols), tile, LANES), lambda i: (0, block * tiles + i, 0))
        for cols in out_columns
    ]
    heads = sum(len(cols) for cols in columns)
    return pl.pallas_call(
        functools.partial(
            cut_kernel,
            kinds=kinds,
            columns=columns,
            roped=rope is not None,
            chained=earlier is not None,
        ),
        grid=(tiles,),
        in_specs=in_specs,
        out_specs=out_specs,
        out_shape=out_shape,
        input_output_aliases=aliases,
        compiler_params=params("arbitrary"),
        cost_estimate=effort(heads * rows * 4.8e-4),
        name="cut_heads",
    )(*operands)


def join_kernel(*refs, kinds, columns, roped):
    gain_ref = refs[0]
    place = 1
    if roped:
        rope_ref = refs[place]
        place += 1
    grads = refs[place : place + len(kinds)]
    place += len(kinds)
    normed_kinds = [number for number, kind in enumerate(kinds) if kind != "v"]
    keeps = dict(zip(normed_kinds, refs[place : place + len(normed_kinds)]))
    out_ref, sum_ref = refs[place + len(normed_kinds) :]
    rows = out_ref.shape[0]
    part = min(256, rows)
    inside = lanes_of((part, LANES)) < HEAD_DIM

    @pl.when(pl.program_id(0) == 0)
    def _():
        sum_ref[...] = jnp.zeros_like(sum_ref)

    def rows_of(span):
        rope = rope_ref[span, :] if roped else None
        pieces = {}
        for number, kind in enumerate(kinds):
            total = jnp.zeros((part, LANES), jnp.float32)
            for head, offset in enumerate(columns[number]):
                slope = grads[number][head, span, :].astype(jnp.float32)
                if kind != "v":
                    slope = jnp.where(inside, slope, 0.0)
                    slope = slope * (SCALE if kind == "q" else KEY_BACK)
                    if roped:
                        slope = turn_back(slope, rope)
                    normed = keeps[number][head, span, :].astype(jnp.float32)
                    spread = (
                        normed[:, HEAD_DIM : HEAD_DIM + 1]
                        + normed[:, HEAD_DIM + 1 : HEAD_DIM + 2]
                    )
                    product = slope * normed
                    total = total + product
                    gain = gain_ref[number : number + 1, :]
                    slope = slope * gain
                    mean = lane_mean(slope, True)
                    mixed = lane_mean(product * gain, False)
                    slope = (slope - mean - normed * mixed) * spread
                pieces[offset] = slope[:, :HEAD_DIM]
            if kind != "v":
                sum_ref[number : number + 1, :] += jnp.sum(total, 0, keepdims=True)
        out_ref[span, :] = jnp.concatenate(
            [pieces[offset] for offset in sorted(pieces)], 1
        ).astype(jnp.bfloat16)

    by_parts(rows, part, rows_of)


def join_heads(keeps, gains, kinds, columns, grads, rope=None, block=0, blocks=1):
    rows = keeps[0].shape[1] // blocks
    width = HEAD_DIM * sum(len(cols) for cols in columns)
    tile = min(256, rows)
    tiles = rows // tile
    operands = [gains]
    in_specs = [pl.BlockSpec((8, LANES), lambda i: (0, 0))]
    if rope is not None:
        operands.append(rope)
        in_specs.append(pl.BlockSpec((tile, 3 * LANES), lambda i: (block * tiles + i, 0)))
    for array in list(grads) + list(keeps):
        operands.append(array)
        in_specs.append(
            pl.BlockSpec((array.shape[0], tile, LANES), lambda i: (0, block * tiles + i, 0))
        )
    heads = sum(len(cols) for cols in columns)
    return pl.pallas_call(
        functools.partial(join_kernel, kinds=kinds, columns=columns, roped=rope is not None),
        grid=(tiles,),
        in_specs=in_specs,
        out_specs=[
            pl.BlockSpec((tile, width), lambda i: (i, 0)),
            pl.BlockSpec((8, LANES), lambda i: (0, 0)),
        ],
        out_shape=[
            jax.ShapeDtypeStruct((rows, width), jnp.bfloat16),
            jax.ShapeDtypeStruct((8, LANES), jnp.float32),
        ],
        compiler_params=params("arbitrary"),
        cost_estimate=effort(heads * rows * 9e-4),
        name="join_heads",
    )(*operands)


def attend_kernel(pick, q_ref, k_ref, v_ref, *refs, steps):
    o_ref, qx_ref = refs[-2:]
    step = pl.program_id(1)
    each, rows, _ = q_ref.shape
    part = min(256, rows)
    for start in range(0, rows, part):
        span = slice(start, start + part)
        merged = []
        for head in range(each):
            queries = q_ref[head, span, :]
            scores = lax.dot_general(
                queries, k_ref[head], ROW_TIMES_ROW, preferred_element_type=jnp.float32
            )
            weights = jnp.exp2(scores).astype(jnp.bfloat16)
            outputs = jnp.dot(weights, v_ref[head], preferred_element_type=jnp.float32)
            total = outputs[:, HEAD_DIM : HEAD_DIM + 1]
            merged.append((outputs * (1.0 / total))[:, :HEAD_DIM])
            level = -jnp.log2(total)
            high = level.astype(jnp.bfloat16).astype(jnp.float32)
            lane = lanes_of(outputs.shape)
            queries = queries.astype(jnp.float32)
            queries = jnp.where(lane == HEAD_DIM + 4, high, queries)
            queries = jnp.where(lane == HEAD_DIM + 5, level - high, queries)
            qx_ref[head, span, :] = queries.astype(jnp.bfloat16)
        merged = jnp.concatenate(merged, 1).astype(jnp.bfloat16)
        width = each * HEAD_DIM
        for number in range(steps):

            @pl.when(step == number)
            def _():
                o_ref[span, number * width : (number + 1) * width] = merged


def attend(queries, keys, values, pick, tile, key_rows, block=0, blocks=1, earlier=None):
    heads, rows_all, _ = queries.shape
    rows = rows_all // blocks
    tiles = rows // tile
    each = 4 if heads % 4 == 0 else 1
    there = lambda i, h, pick: (h, block * tiles + i, 0)
    keyed = lambda i, h, pick: (h, pick[i], 0)
    chained = [] if earlier is None else [earlier]
    return pl.pallas_call(
        functools.partial(attend_kernel, steps=heads // each),
        grid_spec=pltpu.PrefetchScalarGridSpec(
            num_scalar_prefetch=1,
            grid=(tiles, heads // each),
            in_specs=[
                pl.BlockSpec((each, tile, LANES), there),
                pl.BlockSpec((each, key_rows, LANES), keyed),
                pl.BlockSpec((each, key_rows, LANES), keyed),
            ]
            + [pl.BlockSpec(memory_space=pl.ANY)] * len(chained),
            out_specs=[
                pl.BlockSpec((tile, heads * HEAD_DIM), lambda i, h, pick: (i, 0)),
                pl.BlockSpec((each, tile, LANES), there),
            ],
        ),
        out_shape=[
            jax.ShapeDtypeStruct((rows, heads * HEAD_DIM), jnp.bfloat16),
            jax.ShapeDtypeStruct((heads, rows_all, LANES), jnp.bfloat16),
        ],
        input_output_aliases={4: 1} if chained else {},
        compiler_params=params("arbitrary", "arbitrary"),
        cost_estimate=effort(heads * rows * key_rows * 2.5e-6),
        name="attend",
    )(pick, queries, keys, values, *chained)


def cut_grad_kernel(*refs, heads):
    grad_ref, o_ref = refs[:2]
    out_ref = refs[-1]
    rows = grad_ref.shape[0]
    lane = lanes_of((rows, LANES))
    for head in range(heads):
        span = slice(head * HEAD_DIM, (head + 1) * HEAD_DIM)
        slope = grad_ref[:, span].astype(jnp.bfloat16).astype(jnp.float32)
        level = -jnp.sum(slope * o_ref[:, span].astype(jnp.float32), 1, keepdims=True)
        high = level.astype(jnp.bfloat16).astype(jnp.float32)
        slope = widen(slope)
        slope = jnp.where(lane == HEAD_DIM, high, slope)
        slope = jnp.where(lane == HEAD_DIM + 1, level - high, slope)
        out_ref[head] = slope.astype(jnp.bfloat16)


def cut_grad(grad, outputs, block=0, blocks=1, earlier=None):
    rows, width = grad.shape
    heads = width // HEAD_DIM
    tile = min(256, rows)
    tiles = rows // tile
    operands = [grad, outputs]
    in_specs = [pl.BlockSpec((tile, width), lambda i: (i, 0))] * 2
    aliases = {}
    if earlier is not None:
        aliases = {2: 0}
        operands.append(earlier)
        in_specs.append(pl.BlockSpec(memory_space=pl.ANY))
    return pl.pallas_call(
        functools.partial(cut_grad_kernel, heads=heads),
        grid=(tiles,),
        in_specs=in_specs,
        out_specs=pl.BlockSpec((heads, tile, LANES), lambda i: (0, block * tiles + i, 0)),
        out_shape=jax.ShapeDtypeStruct((heads, blocks * rows, LANES), jnp.bfloat16),
        input_output_aliases=aliases,
        compiler_params=params("arbitrary"),
        cost_estimate=effort(heads * rows * 6.5e-4),
        name="cut_grad",
    )(*operands)


def attend_back_kernel(
    pick, q_ref, k_ref, v_ref, g_ref, dq_ref, dk_ref, dv_ref, key_sum, value_sum, *, key_rows
):
    tile = pl.program_id(1)

    @pl.when(tile == 0)
    def _():
        key_sum[...] = jnp.zeros_like(key_sum)
        value_sum[...] = jnp.zeros_like(value_sum)

    start = pl.multiple_of(pick[tile] * key_rows, key_rows)
    for head in range(q_ref.shape[0]):
        queries, keys, slopes = q_ref[head], k_ref[head], g_ref[head]
        scores = lax.dot_general(keys, queries, ROW_TIMES_ROW, preferred_element_type=jnp.float32)
        weights = jnp.exp2(scores)
        pulls = lax.dot_general(
            v_ref[head], slopes, ROW_TIMES_ROW, preferred_element_type=jnp.float32
        )
        pulls = (weights * pulls).astype(jnp.bfloat16)
        value_sum[head, pl.ds(start, key_rows), :] += jnp.dot(
            weights.astype(jnp.bfloat16), slopes, preferred_element_type=jnp.float32
        )
        key_sum[head, pl.ds(start, key_rows), :] += jnp.dot(
            pulls, queries, preferred_element_type=jnp.float32
        )
        query_grad = lax.dot_general(
            pulls, keys, COL_TIMES_COL, preferred_element_type=jnp.float32
        )
        dq_ref[head] = query_grad.astype(jnp.bfloat16)

    @pl.when(tile == pl.num_programs(1) - 1)
    def _():
        dk_ref[...] = key_sum[...].astype(jnp.bfloat16)
        dv_ref[...] = value_sum[...].astype(jnp.bfloat16)


def attend_back(queries, keys, values, slopes, pick, tile, key_rows):
    heads, rows, _ = queries.shape
    all_keys = keys.shape[1]
    tiles = rows // tile
    each = EACH_BACK if heads % EACH_BACK == 0 else 1
    there = lambda h, i, pick: (h, i, 0)
    keyed = lambda h, i, pick: (h, pick[i], 0)
    whole = lambda h, i, pick: (h, 0, 0)
    return pl.pallas_call(
        functools.partial(attend_back_kernel, key_rows=key_rows),
        grid_spec=pltpu.PrefetchScalarGridSpec(
            num_scalar_prefetch=1,
            grid=(heads // each, tiles),
            in_specs=[
                pl.BlockSpec((each, tile, LANES), there),
                pl.BlockSpec((each, key_rows, LANES), keyed),
                pl.BlockSpec((each, key_rows, LANES), keyed),
                pl.BlockSpec((each, tile, LANES), there),
            ],
            out_specs=[
                pl.BlockSpec((each, tile, LANES), there),
                pl.BlockSpec((each, all_keys, LANES), whole),
                pl.BlockSpec((each, all_keys, LANES), whole),
            ],
            scratch_shapes=[pltpu.VMEM((each, all_keys, LANES), jnp.float32)] * 2,
        ),
        out_shape=[
            jax.ShapeDtypeStruct((heads, rows, LANES), jnp.bfloat16),
            jax.ShapeDtypeStruct((heads, all_keys, LANES), jnp.bfloat16),
            jax.ShapeDtypeStruct((heads, all_keys, LANES), jnp.bfloat16),
        ],
        compiler_params=params("arbitrary", "arbitrary"),
        cost_estimate=effort(heads * rows * key_rows * 3.5e-6),
        name="attend_back",
    )(pick, queries, keys, values, slopes)


def sum_product_kernel(*refs, blocks):
    lefts, rights, out_ref = refs[:blocks], refs[blocks : 2 * blocks], refs[-1]
    total = None
    for left, right in zip(lefts, rights):
        term = lax.dot_general(
            left[...], right[...], COL_TIMES_COL, preferred_element_type=jnp.float32
        )
        total = term if total is None else total + term
    out_ref[0] = total.astype(jnp.bfloat16)


def sum_product(lefts, rights, slot=0, slots=1, earlier=None):
    rows, depth = lefts[0].shape
    width = rights[0].shape[1]
    tile = min(512, width)
    blocks = len(lefts)
    chained = [] if earlier is None else [earlier]
    return pl.pallas_call(
        functools.partial(sum_product_kernel, blocks=blocks),
        grid=(pl.cdiv(width, tile),),
        in_specs=[pl.BlockSpec((rows, depth), lambda i: (0, 0))] * blocks
        + [pl.BlockSpec((rows, tile), lambda i: (0, i))] * blocks
        + [pl.BlockSpec(memory_space=pl.ANY)] * len(chained),
        out_specs=pl.BlockSpec((1, depth, tile), lambda i: (slot, 0, i)),
        out_shape=jax.ShapeDtypeStruct((slots, depth, width), jnp.bfloat16),
        input_output_aliases={2 * blocks: 0} if chained else {},
        compiler_params=params("arbitrary"),
        cost_estimate=effort(1 + 2 * blocks * rows * depth * width / 750e6),
        name="sum_product",
    )(*lefts, *rights, *chained)


def product_kernel(*refs, form):
    *terms, out_ref = refs
    half = len(terms) // 2
    total = None
    for left, right in zip(terms[:half], terms[half:]):
        term = lax.dot_general(
            left[...], right[...], form, preferred_element_type=jnp.float32
        )
        total = term if total is None else total + term
    out_ref[...] = total.astype(out_ref.dtype)


PLAIN = (((1,), (0,)), ((), ()))


def tile_of(width):
    for tile in (1024, 768, 1408, 512):
        if width % tile == 0:
            return tile
    return width if width < 1024 else 768


def right_spec(depth, tile, form):
    if form == PLAIN:
        return pl.BlockSpec((depth, tile), lambda i: (0, i))
    return pl.BlockSpec((tile, depth), lambda i: (i, 0))


def product(lefts, rights, form=PLAIN, kind=jnp.bfloat16):
    rows = lefts[0].shape[0]
    width = rights[0].shape[1 if form == PLAIN else 0]
    tile = tile_of(width)
    return pl.pallas_call(
        functools.partial(product_kernel, form=form),
        grid=(pl.cdiv(width, tile),),
        in_specs=[pl.BlockSpec(left.shape, lambda i: (0, 0)) for left in lefts]
        + [right_spec(left.shape[1], tile, form) for left in lefts],
        out_specs=pl.BlockSpec((rows, tile), lambda i: (0, i)),
        out_shape=jax.ShapeDtypeStruct((rows, width), kind),
        compiler_params=params("arbitrary"),
        cost_estimate=effort(1 + 2 * rows * width * sum(left.shape[1] for left in lefts) / 700e6),
        name="product",
    )(*lefts, *rights)


def gelu_kernel(rows_ref, weight_ref, slope_ref, active_ref, grad_ref):
    values = jnp.dot(rows_ref[...], weight_ref[...], preferred_element_type=jnp.float32)
    outer = 0.7978845608028654
    inner = 0.044715
    square = values * values
    bend = jnp.tanh(values * (outer + (outer * inner) * square))
    half = 0.5 + 0.5 * bend
    active_ref[...] = (values * half).astype(jnp.bfloat16)
    rise = (0.5 * outer + (1.5 * outer * inner) * square) * values
    slope = half + rise * (1.0 - bend * bend)
    grad_ref[...] = (slope_ref[...].astype(jnp.float32) * slope).astype(jnp.bfloat16)


def gelu_both(values, weight, slopes):
    rows, depth = values.shape
    width = weight.shape[1]
    tile = 512 if width % 512 == 0 else width
    return pl.pallas_call(
        gelu_kernel,
        grid=(width // tile,),
        in_specs=[
            pl.BlockSpec((rows, depth), lambda i: (0, 0)),
            pl.BlockSpec((depth, tile), lambda i: (0, i)),
            pl.BlockSpec((rows, tile), lambda i: (0, i)),
        ],
        out_specs=[pl.BlockSpec((rows, tile), lambda i: (0, i))] * 2,
        out_shape=[jax.ShapeDtypeStruct((rows, width), jnp.bfloat16)] * 2,
        compiler_params=params("arbitrary"),
        cost_estimate=effort(11),
        name="gelu_both",
    )(values, weight, slopes)


def row_mean(values):
    return jnp.mean(values, 1, keepdims=True)


def norm_rows(values):
    centre = values - row_mean(values)
    spread = lax.rsqrt(row_mean(centre * centre) + EPSILON)
    return centre * spread, spread


def norm_back(slope, normed, spread):
    return (slope - row_mean(slope) - normed * row_mean(slope * normed)) * spread


def sum_refs(refs):
    total = refs[0][...].astype(jnp.float32)
    for ref in refs[1:]:
        total = total + ref[...].astype(jnp.float32)
    return total


def add_gain_sum(ref, values, row=0):
    @pl.when(pl.program_id(0) == 0)
    def _():
        ref[row : row + 1, :] = jnp.zeros_like(ref[row : row + 1, :])

    ref[row : row + 1, :] += jnp.sum(values, 0, keepdims=True)


def first_norms_kernel(slots, hidden_ref, gains_ref, shifts_ref, residual_ref, normed_ref):
    slot = slots[pl.program_id(0)]
    normed, _ = norm_rows(hidden_ref[...])
    residual = normed * gains_ref[0:1, :]
    residual_ref[...] = residual
    again, _ = norm_rows(residual)
    shifted = again * gains_ref[1:2, :] + shifts_ref[pl.ds(slot, 1), :]
    normed_ref[...] = shifted.astype(jnp.bfloat16)


def add_norm_kernel(*refs):
    *terms, gain_ref, residual_ref, normed_ref = refs
    residual = sum_refs(terms)
    residual_ref[...] = residual
    normed, _ = norm_rows(residual)
    normed_ref[...] = (normed * gain_ref[0:1, :]).astype(jnp.bfloat16)


def norm_back_kernel(*refs):
    base_ref, residual_ref, *terms, gain_ref, grad_ref, low_ref, sum_ref = refs
    slope = sum_refs(terms)
    normed, spread = norm_rows(residual_ref[...])
    add_gain_sum(sum_ref, slope * normed)
    grad = base_ref[...].astype(jnp.float32)
    grad = grad + norm_back(slope * gain_ref[0:1, :], normed, spread)
    grad_ref[...] = grad
    low_ref[...] = grad.astype(jnp.bfloat16)


def first_norms_back_kernel(*refs):
    base_ref, hidden_ref, *terms, gains_ref, low_ref, sum_ref, slot_ref = refs
    slope = sum_refs(terms)
    normed, spread = norm_rows(hidden_ref[...])
    again, spread_again = norm_rows(normed * gains_ref[0:1, :])
    add_gain_sum(sum_ref, slope * again, 1)
    slot_ref[...] = jnp.broadcast_to(jnp.sum(slope, 0, keepdims=True), slot_ref.shape)
    slope = base_ref[...] + norm_back(slope * gains_ref[1:2, :], again, spread_again)
    add_gain_sum(sum_ref, slope * normed, 0)
    low_ref[...] = norm_back(slope * gains_ref[0:1, :], normed, spread).astype(jnp.bfloat16)


def row_call(kernel, name, tile, arrays, tables, outs, prefetch=None):
    rows, width = arrays[0].shape
    tiles = rows // tile
    scalars = [] if prefetch is None else [prefetch]
    by_tile = pl.BlockSpec((tile, width), lambda i, *_: (i, 0))
    out_specs, out_shape = [], []
    for out in outs:
        if out == "tile":
            out_specs.append(pl.BlockSpec((8, width), lambda i, *_: (i, 0)))
            out_shape.append(jax.ShapeDtypeStruct((8 * tiles, width), jnp.float32))
        elif isinstance(out, int):
            out_specs.append(pl.BlockSpec((out, width), lambda i, *_: (0, 0)))
            out_shape.append(jax.ShapeDtypeStruct((out, width), jnp.float32))
        else:
            out_specs.append(by_tile)
            out_shape.append(jax.ShapeDtypeStruct((rows, width), out))
    return pl.pallas_call(
        kernel,
        grid_spec=pltpu.PrefetchScalarGridSpec(
            num_scalar_prefetch=len(scalars),
            grid=(tiles,),
            in_specs=[by_tile] * len(arrays)
            + [pl.BlockSpec(table.shape, lambda i, *_: (0, 0)) for table in tables],
            out_specs=out_specs,
        ),
        out_shape=out_shape,
        compiler_params=params("arbitrary"),
        cost_estimate=effort(4),
        name=name,
    )(*scalars, *arrays, *tables)


def dot_rows(left, right):
    return lax.dot_general(left, right, ROW_TIMES_ROW, preferred_element_type=jnp.float32)


def dot_sum(left, right):
    return lax.dot_general(left, right, COL_TIMES_COL, preferred_element_type=jnp.float32)


def dot_plain(left, right):
    return jnp.dot(left, right, preferred_element_type=jnp.float32)


def low(values):
    return values.astype(jnp.bfloat16)


def wide(values):
    return values.astype(jnp.float32)


def after(values, *earlier):
    return lax.optimization_barrier((values,) + earlier)[0]


def from_back(values, step):
    size = lax.axis_size("seq")
    return lax.ppermute(values, "seq", [(i, (i + step) % size) for i in range(size)])


def to_back(values, step):
    size = lax.axis_size("seq")
    return lax.ppermute(values, "seq", [(i, (i - step) % size) for i in range(size)])


def gather_blocks(values):
    return [values] + [from_back(values, step) for step in range(1, lax.axis_size("seq"))]


def send_terms(terms):
    came = [to_back(terms[step], step) for step in range(1, len(terms))]
    if len(came) < 2:
        return came
    total = wide(came[0])
    for one in came[1:]:
        total = total + wide(one)
    return [total]


def row_spans(rows, *shares):
    edges, total = [0], 0
    for share in shares[:-1]:
        total += share
        edges.append(rows * total // sum(shares) // 16 * 16)
    edges.append(rows)
    return [(start, end) for start, end in zip(edges[:-1], edges[1:]) if end > start]


def sum_blocks(terms):
    total = wide(terms[0])
    for one in send_terms([None] + [low(term) for term in terms[1:]]):
        total = total + wide(one)
    return total


def swap_bit(values, axis, bit):
    size = lax.axis_size(axis)
    return lax.ppermute(values, axis, [(i, i ^ (1 << bit)) for i in range(size)])


def power_of_two(axis):
    size = lax.axis_size(axis)
    return size & (size - 1) == 0


def sum_over(values, axis):
    if not power_of_two(axis):
        return lax.psum(values, axis)
    for bit in range(lax.axis_size(axis).bit_length() - 1):
        values = values + swap_bit(values, axis, bit)
    return values


def unsigned(value):
    return value.astype(jnp.uint32)


def cut_at(values, start, size, axis):
    starts = [np.uint32(0)] * values.ndim
    starts[axis] = start
    sizes = list(values.shape)
    sizes[axis] = size
    return lax.dynamic_slice(values, starts, sizes)


def pick_at(values, index, axis):
    return lax.squeeze(cut_at(values, index, 1, axis), [axis])


class Places:
    def __init__(self, **numbers):
        names = list(numbers)
        leaves, tree = jax.tree.flatten([numbers[name] for name in names])
        self.all = lax.optimization_barrier(tuple(leaves))
        for name, value in zip(names, jax.tree.unflatten(tree, self.all)):
            setattr(self, name, value)


def bits_of(axis):
    place = lax.axis_index(axis)
    bits = [(place >> bit) & 1 for bit in range(lax.axis_size(axis).bit_length() - 1)]
    return [(unsigned(bit), unsigned(1 - bit), bit == 0) for bit in bits]


def gather_step(values, came, bit, spot):
    return jnp.where(
        spot.bits[bit][2],
        jnp.concatenate([values, came], 0),
        jnp.concatenate([came, values], 0),
    )


def gather_rows(values, axis, spot):
    if not power_of_two(axis):
        return lax.all_gather(values, axis, axis=0, tiled=True)
    for bit in range(lax.axis_size(axis).bit_length() - 1):
        values = gather_step(values, swap_bit(values, axis, bit), bit, spot)
    return values


def send_piece(half, spot):
    piece = pick_at(half.reshape(lax.axis_size("dp"), -1, half.shape[1]), spot.place, 0)
    return [from_back(piece, step) for step in range(1, lax.axis_size("seq"))]


def core_half(half, spot):
    return pick_at(half.reshape(2, -1, half.shape[1]), spot.bits[0][0], 0)


def join_halves(mine, other, spot):
    return jnp.where(
        spot.bits[0][2],
        jnp.concatenate([mine, other], 0),
        jnp.concatenate([other, mine], 0),
    )


def scatter_rows(grad):
    return lax.psum_scatter(grad[0], "dp", scatter_dimension=0, tiled=True)


class Summing:
    def __init__(self, grad, spot, high_first=False):
        self.parts = lax.axis_size("dp")
        self.top = self.parts.bit_length() - 2
        self.spot = spot
        self.groups, self.width = grad.shape[0], grad.shape[2]
        self.rows = grad.shape[1] // self.parts
        self.bits = list(range(1, self.top))
        if high_first:
            self.bits.reverse()
        self.left = list(range(self.top - 1, 0, -1))
        self.stage = -1
        self.grad = grad

    def split(self, held, axis, bit):
        mine, other, _ = self.spot.bits[bit]
        self.keep, self.sent = pick_at(held, mine, axis), pick_at(held, other, axis)

    def advance(self, *hold):
        if self.stage < 0:
            self.stage = 0
            grad = after(self.grad, *hold) if hold else self.grad
            self.split(grad.reshape(self.groups, 2, -1, self.width), 1, 0)
            self.came = swap_bit(self.sent, "dp", 0)
            return self
        held = self.keep + (after(self.came, *hold) if hold else self.came)
        if self.stage == 0:
            bits = (2,) * (self.top - 1)
            held = held.reshape((self.groups,) + bits + (2 * self.rows, self.width))
        self.stage += 1
        if self.bits:
            bit = self.bits.pop(0)
            axis = self.left.index(bit)
            self.left.remove(bit)
            self.split(held, axis + 1, bit)
            self.came = swap_bit(self.sent, "dp", bit)
        elif self.stage == self.top:
            senders = [i for i in range(self.parts) if (i >> self.top) != (i & 1)]
            self.keep = self.sent = held
            self.came = lax.ppermute(held, "dp", [(i, i ^ (1 << self.top)) for i in senders])
        else:
            owners = [i for i in range(self.parts) if (i >> self.top) == (i & 1)]
            self.split(held.reshape(self.groups, 2, self.rows, self.width), 1, 0)
            self.came = lax.ppermute(self.sent, "dp", [(i, i ^ 1) for i in owners])
        return self

    def fork(self):
        forks = []
        for group in range(self.groups):
            one = copy.copy(self)
            one.groups, one.bits, one.left = 1, list(self.bits), list(self.left)
            one.keep, one.came = self.keep[group : group + 1], self.came[group : group + 1]
            forks.append(one)
        return forks

    def finish(self, *hold):
        while self.stage <= self.top:
            self.advance(*hold)
            hold = ()
        came = after(self.came, *hold) if hold else self.came
        return wide(jnp.where(self.spot.owns, self.keep, came))


def advance_all(sums, *hold):
    for one in sums:
        one.advance(*hold)
        hold = (one.sent,)
    return hold[0]


def rope_table(rows, cols):
    quarter = HEAD_DIM // 4
    lane = jnp.arange(LANES, dtype=jnp.int32)
    rates = jnp.exp(
        -math.log(10000.0) * (lane % quarter).astype(jnp.float32) / quarter
    )
    angles = jnp.arange(SIDE, dtype=jnp.float32)[:, None] * rates[None, :]
    cosine, sine = jnp.cos(angles), jnp.sin(angles)
    leading = (lane // quarter) % 2 == 0
    table = jnp.concatenate(
        [cosine, jnp.where(leading, -sine, 0.0), jnp.where(leading, 0.0, sine)], 1
    )
    lane = jnp.tile(lane, 3)
    by_row = jnp.where(lane < HEAD_DIM // 2, table, 0.0)
    by_col = jnp.where((lane >= HEAD_DIM // 2) & (lane < HEAD_DIM), table, 0.0)
    spots = jnp.arange(SIDE, dtype=jnp.int32)[None, :]
    picks = jnp.concatenate([rows[:, None] == spots, cols[:, None] == spots], 1)
    return jnp.dot(
        picks.astype(jnp.float32), jnp.concatenate([by_row, by_col], 0), precision=PRECISE
    )


def extra_lanes(columns):
    lane = jnp.arange(LANES, dtype=jnp.int32)[None, :]
    table = jnp.zeros((columns[0].shape[0], LANES), jnp.float32)
    for number, column in enumerate(columns):
        table = jnp.where(lane == HEAD_DIM + number, column[:, None], table)
    return table


def gain_rows(*gains):
    stacked = jnp.stack(gains)
    return jnp.pad(stacked, ((0, 8 - len(gains)), (0, LANES - HEAD_DIM)))


def timestep_features(steps, width):
    halfway = width // 2
    rates = jnp.exp(-math.log(10000.0) * jnp.arange(halfway, dtype=jnp.float32) / halfway)
    angles = steps.astype(jnp.float32)[:, None] * rates[None, :]
    return jnp.concatenate([jnp.cos(angles), jnp.sin(angles)], 1)


def on_device(
    latent,
    skip_input,
    clip_text,
    t5_text,
    bucket,
    counts,
    language,
    timesteps,
    cotangent,
    skip_weight,
    skip_gain,
    time_weight,
    shift_weight,
    norm1_gain,
    qkv_weight,
    q_gain,
    k_gain,
    out_weight,
    norm3_gain,
    cross_query,
    cq_gain,
    t5_weight,
    lang_embed,
    cross_kv,
    ck_gain,
    cross_out,
    norm2_gain,
    fc1_weight,
    fc2_weight,
):
    size = lax.axis_size("seq")
    me = lax.axis_index("seq")
    place = lax.axis_index("dp")
    parts = lax.axis_size("dp")
    rows, width = latent.shape
    local_width = out_weight.shape[0]
    local_heads = local_width // HEAD_DIM
    all_heads = local_heads * size
    clip_length, text_local = clip_text.shape[1:]
    text_length = t5_text.shape[1]
    text_width = lang_embed.shape[1]
    tokens = rows * size
    small = (bucket[0] == 1).astype(jnp.int32)
    quarter = tokens // SMALL_PER
    tile = min(quarter, rows)
    slots = max(1, rows // quarter)

    def owner(step):
        return (me - step) % size

    def first_slot(device):
        return small * (device * rows // quarter)

    def slot_places(device):
        found = []
        for slot in range(SMALL_PER):
            offset = slot - first_slot(device)
            inside = (offset >= 0) & (offset < slots)
            found.append((wide(inside), unsigned(jnp.clip(offset, 0, slots - 1))))
        return found

    owners = [owner(step) for step in range(size)]
    ahead = [(me + step) % size for step in range(size)]
    top = parts.bit_length() - 2
    spot = Places(
        place=unsigned(place),
        place_slots=unsigned(place * SMALL_PER),
        place_columns=unsigned(place * (width // parts)),
        bits=bits_of("dp"),
        owns=(place >> top) == (place & 1),
        first=me == 0,
        me_columns=unsigned(me * local_width),
        text_spans=[unsigned(device * text_local) for device in owners],
        joined_spans=[unsigned(device * (2 * width // size)) for device in owners],
        joined_ahead=[unsigned(device * (2 * width // size)) for device in ahead],
        sides=[
            unsigned(side * (width // size)) for side in ((place & 1), 1 - (place & 1))
        ],
        slots_back=[unsigned(first_slot(device)) for device in owners],
        slots_ahead=[unsigned(first_slot(device)) for device in ahead],
        spread=[slot_places(device) for device in ahead],
    )

    order = jnp.concatenate(
        [owner(step) * rows + jnp.arange(rows, dtype=jnp.int32) for step in range(size)]
    )
    slot_of = jnp.where(small == 1, order // quarter, 0)
    within = jnp.where(small == 1, order % quarter, order)
    across = jnp.where(small == 1, SIDE // 2, SIDE)
    rope = rope_table(within // across, within % across)
    own_slots = slot_of[:rows]
    self_extras = dict(
        q=extra_lanes([wide(slot_of == j) for j in range(SMALL_PER)]),
        k=extra_lanes(
            [jnp.where(slot_of == j, 0.0, HIDE) for j in range(SMALL_PER)]
            + [jnp.ones((tokens,), jnp.float32)] * 2
        ),
    )

    qkv_rows = qkv_weight.transpose(1, 2, 0).reshape(3 * local_width, width)
    cq_own = cross_query.T
    kv_own = cross_kv.transpose(1, 2, 0).reshape(2 * local_width, text_width)
    skip_piece = core_half(skip_weight, spot)
    skip_pieces = [from_back(skip_piece, step) for step in range(1, size)]
    active_slopes = [product([cotangent], [fc2_weight], ROW_TIMES_ROW)]
    timesteps = after(timesteps, skip_piece)
    tile_slots = own_slots[::tile]
    slot_masks = wide(tile_slots[:, None] == jnp.arange(SMALL_PER, dtype=jnp.int32)[None, :])
    first_gains = jnp.stack([skip_gain, norm1_gain])
    self_gains = gain_rows(q_gain, k_gain)
    kv_gains = gain_rows(ck_gain, ck_gain)
    query_gains = gain_rows(cq_gain)
    third_gain, second_gain = norm3_gain[None, :], norm2_gain[None, :]
    cross_pick = small * (jnp.arange(rows // tile, dtype=jnp.int32) * tile // quarter)

    my_languages = cut_at(language, spot.slots_back[0], slots, 0)
    words = wide(lang_embed)
    chosen = jnp.where((my_languages == 1)[:, None], words[1][None, :], words[0][None, :])
    my_counts = cut_at(counts, spot.slots_back[0], slots, 0)
    key_place = jnp.arange(KEY_ROWS, dtype=jnp.int32)[None, :]
    visible = jnp.where(
        key_place < text_length,
        key_place < my_counts[:, 1:],
        (key_place - text_length < my_counts[:, :1]) & (key_place < text_length + clip_length),
    ).reshape(-1)
    cross_key_extra = jnp.where(visible, 0.0, HIDE)
    ones_keys = jnp.ones((slots * KEY_ROWS,), jnp.float32)
    zeros_keys = jnp.zeros((slots * KEY_ROWS,), jnp.float32)
    cross_extras = dict(
        q=extra_lanes([jnp.ones((rows,), jnp.float32)]),
        k=extra_lanes([cross_key_extra, zeros_keys, zeros_keys, zeros_keys, ones_keys, ones_keys]),
    )
    tables = [
        *spot.all,
        tile_slots,
        slot_masks,
        first_gains,
        self_gains,
        kv_gains,
        query_gains,
        third_gain,
        second_gain,
        cross_pick,
        chosen,
        *cross_extras.values(),
        *self_extras.values(),
        rope,
    ]

    steps_all = gather_rows(timesteps, "dp", spot)
    features_all = low(timestep_features(steps_all, time_weight.shape[0]))
    gate_all, silu_pull = jax.vjp(jax.nn.silu, dot_plain(features_all, time_weight))
    gate_all = low(gate_all)
    gate = cut_at(gate_all, spot.place_slots, SMALL_PER, 0)
    shift_own = low(dot_plain(gate, shift_weight))
    shift_blocks = gather_blocks(shift_own)
    if size == 2:
        shifts = jnp.where(
            spot.first,
            jnp.concatenate(shift_blocks, 1),
            jnp.concatenate(shift_blocks[::-1], 1),
        )
    else:
        shifts = lax.all_gather(shift_own, "seq", axis=1, tiled=True)

    partial = product([t5_text.reshape(-1, t5_text.shape[2])], [t5_weight])
    partial = partial.reshape(SMALL_PER, text_length, text_width)
    if size == 2:
        chunk = [
            jnp.where(spot.first, latent, skip_input),
            jnp.where(spot.first, skip_input, latent),
        ]
    else:
        joined = jnp.concatenate([latent, skip_input], 1)
        part = 2 * width // size
        chunk = [
            cut_at(joined, spot.joined_spans[step], part, 1) for step in range(size)
        ]
    half_depth = chunk[0].shape[1] // 2
    lefts, rights = [chunk[0]], [skip_weight]
    for step in range(1, size):
        lefts += [cut_at(chunk[step], side, half_depth, 1) for side in spot.sides]
    spare = width - text_width
    cross_rows = jnp.concatenate([cq_own, cross_out, jnp.pad(kv_own, ((0, 0), (0, spare)))], 0)
    cross_pieces = send_piece(after(cross_rows, rope), spot)
    skip_pieces = [
        after(block, partial, shifts, active_slopes[0], cross_rows, *tables, *lefts)
        for block in skip_pieces
    ]
    skip_others = [swap_bit(piece, "dp", 0) for piece in skip_pieces]
    for mine, other in zip(skip_pieces, skip_others):
        rights += [mine, other]


    text_terms = [cut_at(partial, spot.slots_back[step], slots, 0) for step in range(size)]
    text_came = send_terms([after(term, *skip_pieces) for term in text_terms])
    clip_came = []
    for step in range(size):
        block = cut_at(after(clip_text, *skip_pieces), spot.slots_ahead[step], slots, 0)
        clip_came.append(from_back(block, step) if step else block)

    hidden = product(lefts, rights, kind=jnp.float32)
    cross_blocks = [cross_rows] + [
        lax.all_gather(after(piece, hidden), "dp", axis=0, tiled=True) for piece in cross_pieces
    ]
    cq_full = jnp.concatenate([block[:local_width] for block in cross_blocks], 0)
    co_full = jnp.concatenate(
        [block[local_width : 2 * local_width] for block in cross_blocks], 0
    )
    kv_full = jnp.concatenate(
        [block[2 * local_width :, :text_width] for block in cross_blocks], 0
    )
    residual_one, normed = row_call(
        first_norms_kernel,
        "first_norms",
        tile,
        [hidden],
        [first_gains, wide(shifts)],
        [jnp.float32, jnp.bfloat16],
        tile_slots,
    )
    normed_blocks = gather_blocks(normed)


    self_kinds = ("q", "k", "v")
    self_columns = [
        [local_width * which + HEAD_DIM * head for head in range(local_heads)]
        for which in range(3)
    ]
    qkv_blocks, cut = [], None
    for step in range(size):
        qkv_blocks.append(product([normed_blocks[step]], [qkv_rows], ROW_TIMES_ROW))
        if step == 0 and size > 1:
            normed_blocks[1] = after(normed_blocks[1], qkv_blocks[0])
        cut = cut_heads(
            qkv_blocks[step],
            self_gains,
            self_kinds,
            self_columns,
            self_extras,
            rope,
            step,
            size,
            cut,
        )
    queries, keys, values, *self_keeps = cut
    no_pick = jnp.zeros((1,), jnp.int32)
    self_outputs, self_queries = [None] * size, None
    out_terms = [None] * size
    for step in list(range(1, size)) + [0]:
        if step == 0:
            queries = after(queries, *out_terms[1:])
        self_outputs[step], self_queries = attend(
            queries, keys, values, no_pick, rows, tokens, step, size, self_queries
        )
        out_terms[step] = product([self_outputs[step]], [out_weight])
    out_came = send_terms(out_terms)

    hold = out_terms[1:] + text_came + clip_came[1:]
    text_came = [after(came, *hold) for came in text_came]
    clip_came = [after(came, *hold) for came in clip_came]
    projected = wide(text_terms[0])
    for came in text_came:
        projected = projected + wide(came)
    clip_full = jnp.zeros((slots, clip_length, text_width), jnp.bfloat16)
    zero = np.uint32(0)
    for block, span in zip(clip_came, spot.text_spans):
        clip_full = lax.dynamic_update_slice(clip_full, block, [zero, zero, span])
    unused = KEY_ROWS - text_length - clip_length
    context = jnp.concatenate(
        [
            low(projected + chosen[:, None, :]),
            clip_full,
            jnp.zeros((slots, unused, text_width), jnp.bfloat16),
        ],
        1,
    ).reshape(slots * KEY_ROWS, text_width)
    context_kv = product([context], [kv_full], ROW_TIMES_ROW)
    key_columns = [
        2 * local_width * group + HEAD_DIM * head
        for group in range(size)
        for head in range(local_heads)
    ]
    kv_columns = [key_columns, [column + local_width for column in key_columns]]
    cross_keys, cross_values, *kv_keeps = cut_heads(
        context_kv, kv_gains, ("k", "v"), kv_columns, cross_extras
    )

    out_came = [after(came, out_terms[0], cross_keys) for came in out_came]
    cotangent_blocks = gather_blocks(after(cotangent, *out_came))
    residual_two, normed_cross = row_call(
        add_norm_kernel,
        "cross_norm",
        tile,
        [residual_one, out_terms[0], *out_came],
        [third_gain],
        [jnp.float32, jnp.bfloat16],
    )

    cross_pre = product([normed_cross], [cq_full], ROW_TIMES_ROW)
    query_columns = [[HEAD_DIM * head for head in range(all_heads)]]
    cross_queries, *query_keeps = cut_heads(
        cross_pre, query_gains, ("q",), query_columns, cross_extras
    )
    cross_outputs, cross_queries = attend(
        cross_queries, cross_keys, cross_values, cross_pick, tile, KEY_ROWS
    )
    cross_outputs = after(cross_outputs, *cotangent_blocks[1:])
    residual_three, normed_mlp = row_call(
        add_norm_kernel,
        "mlp_norm",
        tile,
        [residual_two, product([cross_outputs], [co_full])],
        [second_gain],
        [jnp.float32, jnp.bfloat16],
    )

    mlp_blocks = gather_blocks(normed_mlp)
    active, expanded_grads, mlp_terms = [], [], []
    for step in range(size):
        gate_out, gate_grad = gelu_both(mlp_blocks[step], fc1_weight, active_slopes[step])
        active.append(gate_out)
        expanded_grads.append(gate_grad)
        mlp_terms.append(product([gate_grad], [fc1_weight], ROW_TIMES_ROW))
        if step == 0:
            fc_terms = [product([active[0]], [fc2_weight])]
            active_slopes += [
                product([block], [fc2_weight], ROW_TIMES_ROW) for block in cotangent_blocks[1:]
            ]
            mlp_blocks[1:] = [
                after(block, mlp_terms[0], fc_terms[0], *active_slopes[1:])
                for block in mlp_blocks[1:]
            ]
    mlp_came = send_terms(mlp_terms)
    fc2_sum = sum_product([after(one, *mlp_terms[1:]) for one in cotangent_blocks], active)
    fc1_sum = sum_product([after(one, fc2_sum) for one in mlp_blocks], expanded_grads)
    for step in range(1, size):
        fc_terms.append(product([after(active[step], fc1_sum)], [fc2_weight]))
    mlp_came = [after(came, fc1_sum, *fc_terms) for came in mlp_came]
    fc2_total = scatter_rows(after(fc2_sum, *mlp_came))
    fc_sums = [Summing(fc1_sum, spot)]
    fc_terms[1:] = [after(term, *mlp_came) for term in fc_terms[1:]]
    fc_came = send_terms(fc_terms)
    joined_blocks = [chunk[0]]
    for step in range(1, size):
        if size == 2:
            block = chunk[1]
        else:
            block = cut_at(joined, spot.joined_ahead[step], part, 1)
        joined_blocks.append(from_back(after(block, *fc_terms), step))

    sent = advance_all(fc_sums, *mlp_came)
    mlp_came = [after(came, sent) for came in mlp_came]
    grad_three, three_low, norm2_sum = row_call(
        norm_back_kernel,
        "mlp_norm_back",
        tile,
        [cotangent, residual_three, mlp_terms[0], *mlp_came],
        [second_gain],
        [jnp.float32, jnp.bfloat16, 8],
    )

    cross_slopes = cut_grad(product([three_low], [co_full], ROW_TIMES_ROW), cross_outputs)
    cross_slopes = after(cross_slopes, advance_all(fc_sums, cross_slopes))
    grad_cq, grad_ck, grad_cv = attend_back(
        cross_queries, cross_keys, cross_values, cross_slopes, cross_pick, tile, KEY_ROWS
    )
    cross_pre_grad, query_sums = join_heads(
        query_keeps, query_gains, ("q",), query_columns, (grad_cq,)
    )
    cross_slope = product([cross_pre_grad], [cq_full])
    fc_came = [after(came, cross_slope) for came in fc_came]
    cross_slope = after(cross_slope, *fc_came, *joined_blocks[1:])
    grad_two, two_low, norm3_sum = row_call(
        norm_back_kernel,
        "cross_norm_back",
        tile,
        [grad_three, residual_two, cross_slope],
        [third_gain],
        [jnp.float32, jnp.bfloat16, 8],
    )
    two_blocks = gather_blocks(two_low)
    block_output = residual_three + wide(fc_terms[0])
    for came in fc_came:
        block_output = block_output + wide(after(came, two_low))
    block_output = low(block_output)
    context_kv_grad, key_sums = join_heads(
        kv_keeps, kv_gains, ("k", "v"), kv_columns, (after(grad_ck, two_low), grad_cv)
    )
    kv_sum = sum_product([context], [context_kv_grad])
    context_grad = product([context_kv_grad], [kv_full], kind=jnp.float32)
    context_grad = context_grad.reshape(slots, KEY_ROWS, text_width)

    def own_part(summed):
        blocks = [
            summed[:, step * (summed.shape[1] // size) : (step + 1) * (summed.shape[1] // size)]
            for step in range(size)
        ]
        return sum_blocks(blocks)

    later = after(three_low, two_low)
    cross_sum = sum_product([later], [cross_outputs], 0, 2)
    cross_sum = sum_product([normed_cross], [cross_pre_grad], 1, 2, cross_sum)
    two_blocks[1:] = [
        after(block, cross_sum, kv_sum, context_grad) for block in two_blocks[1:]
    ]
    cross_sums = [Summing(cross_sum, spot)]
    kv_total = scatter_rows(after(kv_sum, *two_blocks[1:]))
    sent = advance_all(fc_sums + cross_sums, *two_blocks[1:])
    two_blocks[1:] = [after(block, sent) for block in two_blocks[1:]]

    def spread_slots(blocks):
        found = []
        for slot in range(SMALL_PER):
            total = 0.0
            for step, block in enumerate(blocks):
                inside, index = spot.spread[step][slot]
                total = total + inside * wide(pick_at(block, index, 0))
            found.append(total)
        return jnp.stack(found)

    text_grad = context_grad[:, :text_length]
    text_low = after(low(text_grad), *two_blocks[1:])
    text_blocks = [text_low] + [to_back(text_low, step) for step in range(1, size)]
    clip_blocks = []
    for step in range(size):
        block = cut_at(
            context_grad[:, text_length : text_length + clip_length],
            spot.text_spans[step],
            text_local,
            2,
        )
        clip_blocks.append(low(block) if step else block)
    slopes = None
    for step in range(size):
        slopes = cut_grad(
            product([two_blocks[step]], [out_weight], ROW_TIMES_ROW), self_outputs[step], step, size, slopes
        )
    slopes = after(slopes, advance_all(cross_sums, slopes))
    back_tile = min(512, tokens)
    head_grads = attend_back(
        self_queries,
        keys,
        values,
        slopes,
        jnp.zeros((tokens // back_tile,), jnp.int32),
        back_tile,
        tokens,
    )
    sent = advance_all(fc_sums, head_grads[0])
    head_grads = [after(head_grads[0], sent, fc2_total, *text_blocks[1:]), *head_grads[1:]]
    clip_came = [to_back(after(block, sent), step) for step, block in enumerate(clip_blocks)][1:]
    qkv_grads, normed_terms = [None] * size, [None] * size
    self_sums = 0.0
    for step in list(range(1, size)) + [0]:
        if step == 0:
            sent = advance_all(cross_sums, *normed_terms[1:])
            head_grads = [after(head_grads[0], sent), *head_grads[1:]]
        qkv_grads[step], sums = join_heads(
            self_keeps, self_gains, self_kinds, self_columns, head_grads, rope, step, size
        )
        self_sums = self_sums + sums
        normed_terms[step] = product([qkv_grads[step]], [qkv_rows])
    normed_came = send_terms(normed_terms)
    text_blocks[0] = after(text_blocks[0], *normed_terms[1:])
    project_all = low(spread_slots(text_blocks)).reshape(SMALL_PER * text_length, text_width)
    t5_sum = sum_product([project_all], [t5_text.reshape(-1, t5_text.shape[2])])
    out_sum = sum_product(after(two_blocks, t5_sum), self_outputs)
    qkv_sum = sum_product(normed_blocks, qkv_grads)
    normed_terms[0] = after(normed_terms[0], qkv_sum, out_sum)
    normed_came = [after(came, normed_terms[0]) for came in normed_came]
    clip_blocks[1:] = [after(came, normed_terms[0]) for came in clip_came]
    t5_sums, out_sums = [Summing(t5_sum, spot, True)], [Summing(out_sum, spot)]
    qkv_total = scatter_rows(after(qkv_sum, *normed_came))
    sent = advance_all(t5_sums + out_sums + fc_sums, *normed_came)
    normed_came = [after(came, sent, *clip_blocks[1:]) for came in normed_came]

    hidden_low, first_sums, slot_sums = row_call(
        first_norms_back_kernel,
        "first_norms_back",
        tile,
        [grad_two, hidden, normed_terms[0], *normed_came],
        [first_gains],
        [jnp.bfloat16, 8, "tile"],
    )
    hidden_blocks = gather_blocks(hidden_low)
    tongues = wide(my_languages[None, :] == jnp.arange(2, dtype=jnp.int32)[:, None])
    grad_lang = jnp.dot(tongues, jnp.sum(text_grad, 1), precision=PRECISE)
    gains = [
        first_sums[0],
        first_sums[1],
        self_sums[0, :HEAD_DIM],
        self_sums[1, :HEAD_DIM],
        norm3_sum[0],
        query_sums[0, :HEAD_DIM],
        key_sums[0, :HEAD_DIM],
        norm2_sum[0],
        grad_lang.reshape(-1),
    ]
    shift_terms = jnp.zeros((SMALL_PER, width), jnp.float32)
    for number in range(rows // tile):
        shift_terms += slot_masks[number][:, None] * after(slot_sums, hidden_low)[8 * number][None, :]
    flat = jnp.concatenate(gains)
    lines = -(-flat.shape[0] // width)
    flat = jnp.pad(flat, (0, lines * width - flat.shape[0])).reshape(lines, width)
    sent = advance_all(cross_sums + out_sums + t5_sums, shift_terms)
    grad_fc1 = fc_sums[0].finish(sent)[0]
    packed = after(jnp.concatenate([flat, shift_terms], 0), sent, grad_fc1)
    packed_came = swap_bit(packed, "dp", 0)

    def take(packed, came, bit):
        rest = gather_step(packed[lines:], came[lines:], bit, spot)
        return jnp.concatenate([packed[:lines] + came[:lines], rest], 0)

    def next_step(packed, came, bit, hold):
        packed = take(packed, after(came, hold), bit - 1)
        return packed, swap_bit(packed, "dp", bit)

    sent = advance_all(cross_sums + out_sums, packed)
    packed, packed_came = next_step(packed, packed_came, 1, sent)
    hidden_blocks[1:] = [after(block, packed) for block in hidden_blocks[1:]]
    skip_sum = sum_product(hidden_blocks, joined_blocks)
    last_sums = [Summing(skip_sum, spot)]
    sent = advance_all(last_sums, skip_sum)
    packed, packed_came = next_step(packed, packed_came, 2, sent)
    sent = advance_all(last_sums, packed)
    cross_total = cross_sums[0].finish(sent)
    sent = cross_total

    hidden_low = after(hidden_low, sent)
    skip_blocks = [skip_weight]
    for mine, other in zip(skip_pieces, skip_others):
        skip_blocks.append(join_halves(mine, after(other, sent), spot))
    joined_grads = [
        product([hidden_low], [block], ROW_TIMES_ROW, jnp.float32) for block in skip_blocks
    ]
    for bit in range(3, lax.axis_size("dp").bit_length() - 1):
        packed, packed_came = next_step(packed, packed_came, bit, joined_grads)
        joined_grads[0] = after(joined_grads[0], packed)
    sent = advance_all(last_sums + out_sums + t5_sums, *joined_grads)
    project_all = after(project_all, sent)
    grad_t5 = product([project_all], [t5_weight], ROW_TIMES_ROW, jnp.float32)
    grad_t5 = grad_t5.reshape(t5_text.shape)
    sent = grad_t5
    packed = take(packed, after(packed_came, sent), lax.axis_size("dp").bit_length() - 2)
    sent = advance_all(last_sums + out_sums + t5_sums, packed)
    packed = sum_over(after(packed, sent), "seq")
    sent = advance_all(last_sums + t5_sums, packed)
    clip_blocks[0] = after(clip_blocks[0], sent)
    grad_clip = spread_slots(clip_blocks)
    if size == 2:
        grad_latent = jnp.where(spot.first, joined_grads[0], joined_grads[1])
        grad_skip_input = jnp.where(spot.first, joined_grads[1], joined_grads[0])
    else:
        joined_grad = jnp.zeros((rows, 2 * width), jnp.float32)
        for step in range(size):
            joined_grad = lax.dynamic_update_slice(
                joined_grad, joined_grads[step], [np.uint32(0), spot.joined_spans[step]]
            )
        grad_latent, grad_skip_input = joined_grad[:, :width], joined_grad[:, width:]

    flat, totals, start = packed[:lines].reshape(-1), [], 0
    for gain in gains:
        totals.append(flat[start : start + gain.shape[0]])
        start += gain.shape[0]
    shift_all = low(packed[lines:])
    shift_mine = cut_at(shift_all, spot.me_columns, local_width, 1)
    gate_mine = cut_at(gate_all, spot.place_columns, width // parts, 1)
    grad_shift = dot_sum(gate_mine, shift_mine)
    (time_slope,) = silu_pull(sum_over(dot_rows(shift_mine, shift_weight), "seq"))
    grad_time = jnp.dot(wide(features_all).T, time_slope, precision=PRECISE)

    grad_out = out_sums[0].finish(grad_shift)[0].T
    grad_t5_weight = t5_sums[0].finish(grad_out)[0].T
    grad_skip_weight = last_sums[0].finish(grad_t5_weight)[0].T
    grad_qkv = wide(after(qkv_total, grad_skip_weight, kv_total)).reshape(-1, 3, local_width)
    grad_fc2 = wide(after(fc2_total, grad_skip_weight)).T
    grad_cross_kv = own_part(wide(after(kv_total, grad_out))).reshape(-1, 2, local_width)
    grad_cross_out = own_part(cross_total[0]).T
    grad_cross_query = own_part(cross_total[1])

    return (
        block_output,
        grad_latent,
        grad_skip_input,
        grad_clip,
        grad_t5,
        grad_skip_weight,
        totals[0],
        grad_time,
        grad_shift,
        totals[1],
        grad_qkv,
        totals[2],
        totals[3],
        grad_out,
        totals[4],
        grad_cross_query,
        totals[5],
        grad_t5_weight,
        totals[8].reshape(lang_embed.shape),
        grad_cross_kv,
        totals[6],
        grad_cross_out,
        totals[7],
        grad_fc1,
        grad_fc2,
    )


def solution(mesh):
    return jax.shard_map(
        on_device,
        mesh=mesh,
        in_specs=(
            P(("dp", "seq"), None),
            P(("dp", "seq"), None),
            P("dp", None, "seq"),
            P("dp", None, "seq"),
            P("dp"),
            P("dp", None),
            P("dp"),
            P("dp"),
            P(("dp", "seq"), None),
            P("seq", None),
            P(),
            P(),
            P(None, "seq"),
            P(),
            P(None, None, "seq"),
            P(),
            P(),
            P("seq", None),
            P(),
            P(None, "seq"),
            P(),
            P("seq", None),
            P(),
            P(None, None, "seq"),
            P(),
            P("seq", None),
            P(),
            P(None, "seq"),
            P("seq", None),
        ),
        out_specs=(
            P(("dp", "seq"), None),
            P(("dp", "seq"), None),
            P(("dp", "seq"), None),
            P("dp", None, "seq"),
            P("dp", None, "seq"),
            P("seq", "dp"),
            P(),
            P(),
            P("dp", "seq"),
            P(),
            P("dp", None, "seq"),
            P(),
            P(),
            P("seq", "dp"),
            P(),
            P("dp", "seq"),
            P(),
            P("seq", "dp"),
            P(),
            P("dp", None, "seq"),
            P(),
            P("seq", "dp"),
            P(),
            P("dp", "seq"),
            P("seq", "dp"),
        ),
        check_vma=False,
    )
```
